32 devices in a mesh: row: 4 (over x, core), col: 8 (over z, y).
Axes of the slice: x: 2, y: 2, z: 4, core: 2. Of those that a mesh axis runs over, the one named last changes fastest.
Arguments:
- ao_ints: bfloat16 [5120, 15360], P(('row', 'col')), may hold values from -6 to 6
- vir_coef: bfloat16 [5120, 128], P(('row', 'col')), may hold values from -0.15625 to 0.15625
- naf_vectors: bfloat16 [15360, 7168], P('row', 'col'), may hold values from -0.046875 to 0.046875
Outputs:
- gram: float32 [15360, 15360], P('row', 'col')
- naf_ints: float32 [128, 7168], P('row', 'col')
The draws below stay inside these ranges and needn't reach their ends.
All inputs are finite; a program needn't handle non-finite values.
Results may differ from the reference program's by a relative error of at most 0.004.
Values may be sent and summed in bfloat16 or wider, within the bound.
No kernel may reach another device: no remote copies, remote signals or barrier semaphores. Data moves between devices by JAX's collectives and lax.ppermute only.
A program may use at most 128 MiB of HBM per device.

```python
import jax
import jax.numpy as jnp

NAO = 5120
NAUX = 15360
NNAF = 7168
VB = 128


def with_spikes(entries, stream_key, source, target, shards_of, factor):
    def block_of(dim):
        return (jnp.arange(entries.shape[dim]) // (entries.shape[dim] // shards_of)).reshape((-1,) + (1,) * (entries.ndim - 1 - dim))

    first = jax.random.permutation(stream_key, shards_of)[block_of(target)]
    other_side = (block_of(target) + shards_of // 2) % shards_of
    return jnp.where((block_of(source) == first) | (block_of(source) == other_side), factor * entries, entries)


def block_scale(stream_key, shape, split, low, largest):
    def one(position, shards_of):
        steps = jax.random.uniform(jax.random.fold_in(jax.random.fold_in(stream_key, 6), position), (shards_of,), jnp.float32, low / len(split), largest / len(split))
        return jnp.repeat(jnp.exp(steps), shape[position] // shards_of).reshape((-1,) + (1,) * (len(shape) - position - 1))

    loudness = one(*split[0])
    for cut in split[1:]:
        loudness = loudness * one(*cut)
    return loudness


def bell_draw(stream_key, dims, width, most, cuts=(), held_as=jnp.bfloat16):
    level = block_scale(stream_key, dims, cuts, -0.22, 0.18) if cuts else 1.0
    result = jax.random.normal(stream_key, dims, jnp.float32) * width * level
    return jnp.minimum(jnp.maximum(result, -most), most).astype(held_as)


def heavy_noise(key, shape, width, most, split, heavy, dtype=jnp.bfloat16):
    values = width * jax.random.normal(key, shape, jnp.float32)
    if split:
        values = values * block_scale(key, shape, split, -0.22, 0.18)
    return jnp.clip(with_spikes(values, jax.random.fold_in(key, 3), *heavy), -most, most).astype(dtype)


def setup_inputs(seed: int = 0) -> dict:
    streams_of = jax.random.split(jax.random.key(seed), 4)
    return {
        "ao_ints": bell_draw(streams_of[0], (NAO, NAUX), 1.0, 6.0, ((0, 32),)),
        "vir_coef": heavy_noise(streams_of[1], (NAO, VB), NAO ** -0.5, 0.15625, ((0, 32),), (0, 1, 32, 2.75)),
        "naf_vectors": bell_draw(streams_of[2], (NAUX, NNAF), NAUX ** -0.5, 0.046875, ((0, 4), (1, 8))),
    }


def reference(ao_ints, vir_coef, naf_vectors):
    half = jnp.dot(vir_coef.T, ao_ints, preferred_element_type=jnp.float32)
    bia = half.astype(jnp.bfloat16)
    gram = jnp.dot(bia.T, bia, preferred_element_type=jnp.float32) * (1.0 / VB)
    naf_ints = jnp.dot(bia, naf_vectors, preferred_element_type=jnp.float32)
    return gram, naf_ints
```

```python
import functools

import jax
import jax.numpy as jnp
from jax import lax
from jax.experimental import pallas as pl
from jax.experimental.pallas import tpu as pltpu
from jax.sharding import PartitionSpec as P

AXES = ("row", "col")
GROUPS = 1
TURNS = 3
HEAD = 16
VMEM_LIMIT = 48 * 2**20


def contract_first(lhs, rhs):
    return lax.dot_general(lhs, rhs, (((0,), (0,)), ((), ())), preferred_element_type=jnp.float32)


def contract_second(lhs, rhs):
    return lax.dot_general(lhs, rhs, (((1,), (1,)), ((), ())), preferred_element_type=jnp.float32)


def shards(ao_ints, vir_coef, naf_vectors):
    n_row = lax.axis_size("row")
    n_col = lax.axis_size("col")
    virtuals = vir_coef.shape[1]
    aux_total = ao_ints.shape[1]
    row_width = aux_total // n_row
    col_width = aux_total // n_col
    row_index = lax.axis_index("row")
    col_index = lax.axis_index("col")
    owned_rows = lax.psum_scatter(
        contract_first(ao_ints, vir_coef), ("row", "col"), scatter_dimension=0, tiled=True
    ).astype(jnp.bfloat16)
    gathered = lax.all_gather(owned_rows, ("row", "col"), axis=0, tiled=True)
    panel_rows = lax.dynamic_slice_in_dim(gathered, row_index * row_width, row_width, 0)
    panel_cols = lax.dynamic_slice_in_dim(gathered, col_index * col_width, col_width, 0)
    tile_sum = contract_second(panel_rows, panel_cols)
    projection = contract_first(panel_rows, naf_vectors)
    naf_ints = lax.psum_scatter(projection, "row", scatter_dimension=0, tiled=True)
    return (tile_sum * (1.0 / virtuals), naf_ints)


ORDERS = (("x", "y", "z0"), ("y", "z0", "x"), ("z0", "x", "y"))
FLIPS = {"core": (1, 0), "x": (2, 0), "y": (0, 1), "z0": (0, 2), "z1": (0, 4), "yz0": (0, 3), "xcore": (3, 0)}


def swap(value, direction):
    over_row, over_col = FLIPS[direction]
    pairs = [(r * 8 + c, (r ^ over_row) * 8 + (c ^ over_col)) for r in range(4) for c in range(8)]
    return lax.ppermute(value, AXES, pairs)


def half_kernel(nb, bits, vir, ao, *outs):
    acc = contract_first(ao[...], vir[...])
    pieces, bound = outs[:-1], outs[-1]
    width = 2 * nb
    for n, out in enumerate(pieces):
        turn, group = divmod(n, GROUPS)
        start = (turn * GROUPS + group) * width
        rows = acc[start : start + width]
        if turn == 0:
            out[0, 0] = rows
        elif turn == 1:
            out[0, 0, 0] = rows[:nb]
            out[0, 1, 0] = rows[nb:]
        else:
            out[0, 0, 0] = rows[:nb]
            out[1, 0, 0] = rows[nb:]
    largest = jnp.max(jnp.max(jnp.abs(acc), axis=0, keepdims=True), axis=1, keepdims=True)
    largest = jnp.broadcast_to(largest, bound.shape)

    @pl.when(pl.program_id(0) == 0)
    def _():
        bound[...] = largest

    @pl.when(pl.program_id(0) > 0)
    def _():
        bound[...] = jnp.maximum(bound[...], largest)


def half_pieces(ao_ints, vir_coef, core):
    naos, aux = ao_ints.shape
    virtuals = vir_coef.shape[1]
    width = aux // 8
    nb = width // (2 * TURNS * GROUPS)
    shapes, specs = [], []
    for turn in range(TURNS):
        if turn == 0:
            shape, block, where = (2, 2, 2 * nb, virtuals), (1, 1, 2 * nb, virtuals), lambda i, b: (i // 2, i % 2, 0, 0)
        elif turn == 1:
            shape, block, where = (2, 2, 2, nb, virtuals), (1, 2, 1, nb, virtuals), lambda i, b: (i % 2, 0, i // 2, 0, 0)
        else:
            shape, block, where = (2, 2, 2, nb, virtuals), (2, 1, 1, nb, virtuals), lambda i, b: (0, i // 2, i % 2, 0, 0)
        shapes += [jax.ShapeDtypeStruct(shape, jnp.float32)] * GROUPS
        specs += [pl.BlockSpec(block, where)] * GROUPS
    shapes.append(jax.ShapeDtypeStruct((8, virtuals), jnp.float32))
    specs.append(pl.BlockSpec((8, virtuals), lambda i, b: (0, 0)))
    *pieces, bound = pl.pallas_call(
        functools.partial(half_kernel, nb),
        grid_spec=pltpu.PrefetchScalarGridSpec(
            num_scalar_prefetch=1,
            grid=(4,),
            in_specs=[
                pl.BlockSpec((naos, virtuals), lambda i, b: (0, 0)),
                pl.BlockSpec((naos, width), lambda i, b: (0, 4 * (i // 2) + 2 * b[0] + i % 2)),
            ],
            out_specs=specs,
        ),
        out_shape=shapes,
        compiler_params=pltpu.CompilerParams(vmem_limit_bytes=VMEM_LIMIT),
    )(core.reshape(1).astype(jnp.int32), vir_coef, ao_ints)
    return [p.reshape(2, 2, 2, nb, virtuals) for p in pieces], bound[:1]


def exponent_of(bound):
    return jnp.ceil(jnp.log2(jnp.maximum(bound, 1e-30))) + 1.0


def packed(value, exponent):
    flat = (value * jnp.exp2(14.0 - exponent)).reshape(-1, value.shape[-1]).astype(jnp.float16)
    head = jnp.broadcast_to(exponent, (HEAD, flat.shape[1])).astype(jnp.float16)
    return jnp.concatenate([flat, head], axis=0)


def opened(message, lead):
    exponent = message[-1:].astype(jnp.float32)
    body = message[:-HEAD]
    return body.reshape(lead + (-1, body.shape[1])), exponent


def pick(array, indices):
    for index in indices:
        array = lax.dynamic_index_in_dim(array, index, 0, keepdims=False)
    return array


def total(sources, indices):
    acc = None
    for array, exponent, taken in sources:
        part = pick(array, indices[taken:])
        if exponent is not None:
            part = part.astype(jnp.float32) * jnp.exp2(exponent - 14.0)
        acc = part if acc is None else acc + part
    return acc


def gram_kernel(nb, scale, bits, own, over_z, over_y, over_yz, col_own, col_other, out, cols):
    step = pl.program_id(0)
    width = 2 * nb

    @pl.when(step == 0)
    def _():
        z0 = bits[1]
        for n in range(TURNS * GROUPS):
            first = pl.multiple_of(n * width + z0 * nb, 16)
            second = pl.multiple_of(n * width + (1 - z0) * nb, 16)
            cols[pl.ds(first, nb), :] = col_own[n * nb : (n + 1) * nb, :]
            cols[pl.ds(second, nb), :] = col_other[n * nb : (n + 1) * nb, :]

    n = TURNS * GROUPS
    for source, rows in enumerate((own, over_z, over_y, over_yz)):

        @pl.when(step // n == source)
        def _(rows=rows):
            start = pl.multiple_of((step % n) * nb, 16)
            out[...] = contract_second(rows[pl.ds(start, nb), :], cols[...]) * scale


def block_of(i, bits):
    n = TURNS * GROUPS
    source = i // n
    y = (bits[0] + source // 2) % 2
    z0 = (bits[1] + source) % 2
    return (y * n + i % n) * 2 + z0


def gram_tile(bits, panels, col_own, col_other, nb):
    rows, virtuals = panels[0].shape
    whole = lambda a: pl.BlockSpec(a.shape, lambda i, b: (0, 0))
    col_width = 2 * rows
    return pl.pallas_call(
        functools.partial(gram_kernel, nb, 1.0 / virtuals),
        grid_spec=pltpu.PrefetchScalarGridSpec(
            num_scalar_prefetch=1,
            grid=(4 * rows // nb,),
            in_specs=[whole(a) for a in (*panels, col_own, col_other)],
            out_specs=pl.BlockSpec((nb, col_width), lambda i, b: (block_of(i, b), 0)),
            scratch_shapes=[pltpu.VMEM((col_width, virtuals), jnp.bfloat16)],
        ),
        out_shape=jax.ShapeDtypeStruct((4 * rows, col_width), jnp.float32),
        compiler_params=pltpu.CompilerParams(vmem_limit_bytes=VMEM_LIMIT),
    )(bits, *panels, col_own, col_other)


def naf_kernel(nb, bits, own, over_z, over_y, over_yz, naf, out):
    step = pl.program_id(0)
    n = TURNS * GROUPS

    @pl.when(step == 0)
    def _():
        out[...] = jnp.zeros_like(out)

    for source, rows in enumerate((own, over_z, over_y, over_yz)):

        @pl.when(step // n == source)
        def _(rows=rows):
            start = pl.multiple_of((step % n) * nb, 16)
            out[...] += contract_first(rows[pl.ds(start, nb), :], naf[...])


def projection_of(bits, panels, naf_vectors, nb):
    rows, virtuals = panels[0].shape
    whole = lambda a: pl.BlockSpec(a.shape, lambda i, b: (0, 0))
    nnaf = naf_vectors.shape[1]
    return pl.pallas_call(
        functools.partial(naf_kernel, nb),
        grid_spec=pltpu.PrefetchScalarGridSpec(
            num_scalar_prefetch=1,
            grid=(4 * rows // nb,),
            in_specs=[whole(a) for a in panels] + [pl.BlockSpec((nb, nnaf), lambda i, b: (block_of(i, b), 0))],
            out_specs=pl.BlockSpec((virtuals, nnaf), lambda i, b: (0, 0)),
        ),
        out_shape=jax.ShapeDtypeStruct((virtuals, nnaf), jnp.float32),
        compiler_params=pltpu.CompilerParams(vmem_limit_bytes=VMEM_LIMIT),
    )(bits, *panels, naf_vectors)


def shards_4x8(ao_ints, vir_coef, naf_vectors):
    virtuals = vir_coef.shape[1]
    row_index = lax.axis_index("row")
    col_index = lax.axis_index("col")
    core = row_index % 2
    place = {"x": row_index // 2, "y": col_index % 2, "z0": col_index // 2 % 2}
    z1 = col_index // 4

    away, away_bound = half_pieces(ao_ints, vir_coef, 1 - core)
    away_exponent = exponent_of(away_bound)
    arrived = [swap(packed(p, away_exponent), "core") for p in away]
    kept, kept_bound = half_pieces(ao_ints, vir_coef, core)
    kept_exponent = exponent_of(kept_bound)
    nb = kept[0].shape[3]

    summed = []
    for n, (keep, message) in enumerate(zip(kept, arrived)):
        order = ORDERS[n // GROUPS]
        body, exponent = opened(message, (2, 2, 2))
        sources = [(keep, None, 0), (body, exponent, 0)]
        level = jnp.maximum(kept_exponent, exponent) + 1.0
        indices = []
        for step, direction in enumerate(order):
            out = packed(total(sources, indices + [1 - place[direction]]), level)
            indices = indices + [place[direction]]
            body, exponent = opened(swap(out, direction), (2,) * (2 - step))
            sources.append((body, exponent, step + 1))
            level = jnp.maximum(level, exponent) + 1.0
        summed.append((total(sources, indices), level))

    blocks = []
    for value, level in summed:
        mine = packed(value, level)
        theirs = swap(mine, "z1")
        parts = [opened(m, ()) for m in (mine, theirs)]
        blocks.append(sum(b.astype(jnp.float32) * jnp.exp2(e - 14.0) for b, e in parts).astype(jnp.bfloat16))
    own = jnp.concatenate(blocks, axis=0)

    over_z = swap(own, "z0")
    over_y = swap(own, "y")
    over_yz = swap(own, "yz0")

    local = jnp.concatenate([own, over_z], axis=0)
    across = [((z // 2 * 2 + z % 2) * 8 + z * 2 + y, ((1 - z // 2) * 2 + z % 2) * 8 + z * 2 + y) for z in range(4) for y in range(2)]
    columns = jnp.where(place["x"] == z1, local, lax.ppermute(local, AXES, across))
    beside = [((x * 2 + z % 2) * 8 + z * 2 + y, (x * 2 + 1 - z % 2) * 8 + z * 2 + y) for x in range(2) for z in range(4) for y in range(2)]
    columns = jnp.where(core == place["z0"], columns, lax.ppermute(columns, AXES, beside))
    rows = own.shape[0]
    col_own, col_other = columns[:rows], columns[rows:]

    bits = jnp.stack([place["y"], place["z0"]]).astype(jnp.int32)
    panels = (own, over_z, over_y, over_yz)
    partial = projection_of(bits, panels, naf_vectors, nb).reshape(4, virtuals // 4, -1)
    naf_ints = pick(partial, [row_index])
    for flip, direction in ((1, "core"), (2, "x"), (3, "xcore")):
        naf_ints = naf_ints + swap(pick(partial, [row_index ^ flip]), direction)
    gram = gram_tile(bits, panels, col_own, col_other, nb)
    return gram, naf_ints


def solution(mesh):
    in_specs = (P(("row", "col"), None), P(("row", "col"), None), P("row", "col"))
    out_specs = (P("row", "col"), P("row", "col"))
    plan = shards_4x8 if (mesh.shape["row"], mesh.shape["col"]) == (4, 8) else shards
    return jax.shard_map(plan, mesh=mesh, in_specs=in_specs, out_specs=out_specs, check_vma=False)
```

```python
import functools

import jax
import jax.numpy as jnp
from jax import lax
from jax.experimental import pallas as pl
from jax.experimental.pallas import tpu as pltpu
from jax.sharding import PartitionSpec as P

AXES = ("row", "col")
TILE = 16
SLOTS = 3
VMEM_LIMIT = 11 * 2**20


def contract_first(lhs, rhs):
    return lax.dot_general(lhs, rhs, (((0,), (0,)), ((), ())), preferred_element_type=jnp.float32)


def contract_second(lhs, rhs):
    return lax.dot_general(lhs, rhs, (((1,), (1,)), ((), ())), preferred_element_type=jnp.float32)


def shards(ao_ints, vir_coef, naf_vectors):
    n_row = lax.axis_size("row")
    n_col = lax.axis_size("col")
    virtuals = vir_coef.shape[1]
    aux_total = ao_ints.shape[1]
    row_width = aux_total // n_row
    col_width = aux_total // n_col
    row_index = lax.axis_index("row")
    col_index = lax.axis_index("col")
    owned_rows = lax.psum_scatter(
        contract_first(ao_ints, vir_coef), ("row", "col"), scatter_dimension=0, tiled=True
    ).astype(jnp.bfloat16)
    gathered = lax.all_gather(owned_rows, ("row", "col"), axis=0, tiled=True)
    panel_rows = lax.dynamic_slice_in_dim(gathered, row_index * row_width, row_width, 0)
    panel_cols = lax.dynamic_slice_in_dim(gathered, col_index * col_width, col_width, 0)
    tile_sum = contract_second(panel_rows, panel_cols)
    projection = contract_first(panel_rows, naf_vectors)
    naf_ints = lax.psum_scatter(projection, "row", scatter_dimension=0, tiled=True)
    return (tile_sum * (1.0 / virtuals), naf_ints)


X, Y, Z0, Z1 = (2, 0), (0, 1), (0, 2), (0, 4)
ORDERS = (((X, Y, Z0), (Y, Z0, X)), ((Z0, X, Y), (Z0, X, Y)))


def flipped(value, on_core0, on_core1):
    pairs = []
    for r in range(4):
        over_row, over_col = on_core1 if r % 2 else on_core0
        pairs += [(r * 8 + c, (r ^ over_row) * 8 + (c ^ over_col)) for c in range(8)]
    return lax.ppermute(value, AXES, pairs)


def half_kernel(sizes, bits, vir, ao, *outs):
    h = pl.program_id(0)
    b = bits[0]
    acc = contract_first(ao[...], vir[...])
    *pieces, bound = outs
    half = acc.shape[0] // 2
    for y in range(2):
        start = y * half
        for piece, (out, rows) in enumerate(zip(pieces, sizes)):
            for z0 in range(2):
                if piece == 0:
                    place = h * (4 - 3 * b) + y * (2 + 2 * b) + z0 * (1 + b)
                else:
                    place = z0 * 4 + h * 2 + y
                tiles = rows // TILE
                value = acc[start : start + rows].reshape(tiles, TILE, acc.shape[1])
                out[pl.ds(place * tiles, tiles)] = value
                start += rows
    largest = jnp.max(jnp.max(jnp.abs(acc), axis=0, keepdims=True), axis=1, keepdims=True)
    largest = jnp.broadcast_to(largest, bound.shape)

    @pl.when(h == 0)
    def _():
        bound[...] = largest
        for out in pieces:
            out[out.shape[0] - 1] = jnp.zeros(out.shape[1:], jnp.float32)

    @pl.when(h > 0)
    def _():
        bound[...] = jnp.maximum(bound[...], largest)


def half_pieces(ao_ints, vir_coef, core, sizes):
    naos, aux = ao_ints.shape
    virtuals = vir_coef.shape[1]
    shapes = [pltpu.VMEM((8 * s // TILE + 1, TILE, virtuals), jnp.float32) for s in sizes]
    shapes.append(pltpu.VMEM((8, virtuals), jnp.float32))
    *pieces, bound = pl.pallas_call(
        functools.partial(half_kernel, sizes),
        grid_spec=pltpu.PrefetchScalarGridSpec(
            num_scalar_prefetch=1,
            grid=(2,),
            in_specs=[
                pl.BlockSpec((naos, virtuals), lambda i, b: (0, 0)),
                pl.BlockSpec((naos, aux // 4), lambda i, b: (0, 2 * i + b[0])),
            ],
            out_specs=[pl.BlockSpec(memory_space=pltpu.VMEM)] * len(shapes),
        ),
        out_shape=shapes,
        compiler_params=pltpu.CompilerParams(vmem_limit_bytes=6 * 2**20),
        cost_estimate=pl.CostEstimate(flops=naos * aux * virtuals, bytes_accessed=naos * aux + 2 * aux * virtuals, transcendentals=0),
    )(core.reshape(1).astype(jnp.int32), vir_coef, pltpu.with_memory_space_constraint(ao_ints, pltpu.HBM))
    return pieces, bound[:1]


def exponent_of(bound):
    return jnp.ceil(jnp.log2(jnp.maximum(bound, 1e-30))) + 1.0


def packed(value, exponent):
    head = lax.broadcasted_iota(jnp.int32, value.shape, 0) == value.shape[0] - 1
    return jnp.where(head, exponent, value * jnp.exp2(14.0 - exponent)).astype(jnp.float16)


def exponent_in(message):
    return message[-1, :1].astype(jnp.float32)


def risen(level, messages):
    for message in messages:
        level = jnp.maximum(level, exponent_in(message))
    return level + 1.0


def joined(kept, message, start, tiles):
    mine = lax.dynamic_slice_in_dim(kept, start, tiles + 1, 0)
    theirs = lax.dynamic_slice_in_dim(message, start, tiles + 1, 0).astype(jnp.float32)
    return mine + theirs * jnp.exp2(exponent_in(message) - 14.0)


def row_start(place, rows, piece, sizes):
    half = 2 * sum(sizes)
    return pl.multiple_of(place // 2 * half + 2 * sum(sizes[:piece]) + place % 2 * rows, TILE)


def blocks_of(sizes, places, array, first, count):
    blocks, at = [], 0
    for n in range(count):
        for piece, rows in enumerate(sizes):
            blocks.append((array, at, rows, row_start(places[first + n], rows, piece, sizes)))
            at += rows
    return blocks


def gram_steps(sizes, scale, blocks, cols, out, buffers, sems):
    rows = sizes[1]
    copies = []
    for ref, at, height, start in blocks:
        for k in range(height // rows):
            n = len(copies)
            if n >= SLOTS:
                copies[n - SLOTS].wait()
            slot = n % SLOTS
            buffers[slot] = contract_second(ref[at + k * rows : at + (k + 1) * rows], cols[...]) * scale
            where = pl.ds(pl.multiple_of(start + k * rows, TILE), rows)
            copies.append(pltpu.make_async_copy(buffers.at[slot], out.at[where, :], sems.at[slot]))
            copies[n].start()
    for copy in copies[-SLOTS:]:
        copy.wait()


def gram_first_kernel(sizes, scale, places, own, near, cols, naf, out, ahead, buffers, sems, naf_sems):
    loads = []
    for n, (_, at, rows, start) in enumerate(blocks_of(sizes, places, ahead, 1, 3)):
        loads.append(pltpu.make_async_copy(naf.at[pl.ds(start, rows), :], ahead.at[pl.ds(at, rows), :], naf_sems.at[n]))
        loads[n].start()
    gram_steps(sizes, scale, blocks_of(sizes, places, own, 0, 1) + blocks_of(sizes, places, near, 1, 1), cols, out, buffers, sems)
    for load in loads:
        load.wait()


def gram_rest_kernel(sizes, scale, places, far, cols, begun, out, buffers, sems):
    gram_steps(sizes, scale, blocks_of(sizes, places, far, 2, 2), cols, out, buffers, sems)


def gram_first(sizes, places, own, near, cols, naf_vectors):
    in_vmem = pl.BlockSpec(memory_space=pltpu.VMEM)
    in_hbm = pl.BlockSpec(memory_space=pl.ANY)
    block, virtuals = own.shape
    nnaf = naf_vectors.shape[1]
    return pl.pallas_call(
        functools.partial(gram_first_kernel, sizes, 1.0 / virtuals),
        grid_spec=pltpu.PrefetchScalarGridSpec(
            num_scalar_prefetch=1,
            grid=(),
            in_specs=[in_vmem, in_vmem, in_vmem, in_hbm],
            out_specs=[in_hbm, in_vmem],
            scratch_shapes=[
                pltpu.VMEM((SLOTS, sizes[1], 2 * block), jnp.float32),
                pltpu.SemaphoreType.DMA((SLOTS,)),
                pltpu.SemaphoreType.DMA((6,)),
            ],
        ),
        out_shape=[
            jax.ShapeDtypeStruct((4 * block, 2 * block), jnp.float32),
            pltpu.VMEM((3 * block, nnaf), jnp.bfloat16),
        ],
        compiler_params=pltpu.CompilerParams(vmem_limit_bytes=VMEM_LIMIT),
        cost_estimate=pl.CostEstimate(flops=8 * block * block * virtuals, bytes_accessed=16 * block * block, transcendentals=0),
    )(places, own, near, cols, pltpu.with_memory_space_constraint(naf_vectors, pltpu.HBM))


def gram_rest(sizes, places, far, cols, begun):
    in_vmem = pl.BlockSpec(memory_space=pltpu.VMEM)
    in_hbm = pl.BlockSpec(memory_space=pl.ANY)
    block, virtuals = far.shape[0] // 2, far.shape[1]
    return pl.pallas_call(
        functools.partial(gram_rest_kernel, sizes, 1.0 / virtuals),
        grid_spec=pltpu.PrefetchScalarGridSpec(
            num_scalar_prefetch=1,
            grid=(),
            in_specs=[in_vmem, in_vmem, in_hbm],
            out_specs=in_hbm,
            scratch_shapes=[pltpu.VMEM((SLOTS, sizes[1], 2 * block), jnp.float32), pltpu.SemaphoreType.DMA((SLOTS,))],
        ),
        out_shape=jax.ShapeDtypeStruct((4 * block, 2 * block), jnp.float32),
        input_output_aliases={3: 0},
        compiler_params=pltpu.CompilerParams(vmem_limit_bytes=VMEM_LIMIT),
        cost_estimate=pl.CostEstimate(flops=8 * block * block * virtuals, bytes_accessed=16 * block * block, transcendentals=0),
    )(places, far, cols, begun)


def naf_first_kernel(sizes, places, own, naf, out, buffer, sems):
    loads = []
    for n, (_, at, rows, start) in enumerate(blocks_of(sizes, places, own, 0, 1)):
        loads.append(pltpu.make_async_copy(naf.at[pl.ds(start, rows), :], buffer.at[pl.ds(at, rows), :], sems.at[n]))
        loads[n].start()
    for load in loads:
        load.wait()
    out[...] = contract_first(own[...], buffer[...])


def naf_first(sizes, places, own, naf_vectors):
    block, virtuals = own.shape
    nnaf = naf_vectors.shape[1]
    in_vmem = pl.BlockSpec(memory_space=pltpu.VMEM)
    return pl.pallas_call(
        functools.partial(naf_first_kernel, sizes),
        grid_spec=pltpu.PrefetchScalarGridSpec(
            num_scalar_prefetch=1,
            grid=(),
            in_specs=[in_vmem, pl.BlockSpec(memory_space=pl.ANY)],
            out_specs=in_vmem,
            scratch_shapes=[pltpu.VMEM((block, nnaf), jnp.bfloat16), pltpu.SemaphoreType.DMA((2,))],
        ),
        out_shape=pltpu.VMEM((virtuals, nnaf), jnp.float32),
        compiler_params=pltpu.CompilerParams(vmem_limit_bytes=VMEM_LIMIT),
        cost_estimate=pl.CostEstimate(flops=2 * block * nnaf * virtuals, bytes_accessed=2 * block * nnaf, transcendentals=0),
    )(places, own, pltpu.with_memory_space_constraint(naf_vectors, pltpu.HBM))


def naf_rest_kernel(near, far, naf, before, out):
    block = near.shape[0]
    out[...] = before[...] + contract_first(near[...], naf[:block]) + contract_first(far[...], naf[block:])


def naf_rest(near, far, naf, before):
    in_vmem = pl.BlockSpec(memory_space=pltpu.VMEM)
    return pl.pallas_call(
        naf_rest_kernel,
        in_specs=[in_vmem] * 4,
        out_specs=in_vmem,
        out_shape=pltpu.VMEM(before.shape, jnp.float32),
        compiler_params=pltpu.CompilerParams(vmem_limit_bytes=5 * 2**20),
        cost_estimate=pl.CostEstimate(flops=2 * naf.shape[0] * before.size, bytes_accessed=0, transcendentals=0),
    )(near, far, naf, before)


def shards_4x8(ao_ints, vir_coef, naf_vectors):
    virtuals = vir_coef.shape[1]
    row_index = lax.axis_index("row")
    col_index = lax.axis_index("col")
    core, x = row_index % 2, row_index // 2
    y, z0, z1 = col_index % 2, col_index // 2 % 2, col_index // 4
    place = {X: x, Y: y, Z0: z0}
    third = ao_ints.shape[1] // 48
    sizes = (2 * third, third)

    away, bound = half_pieces(ao_ints, vir_coef, 1 - core, sizes)
    exponent = exponent_of(bound)
    arrived = [flipped(packed(p, exponent), (1, 0), (1, 0)) for p in away]
    kept, bound = half_pieces(ao_ints, vir_coef, core, sizes)
    exponent = exponent_of(bound)

    level = risen(exponent, arrived)
    tiles = [8 * s // TILE for s in sizes]
    for step in range(3):
        sent, left = [], []
        for piece, orders in enumerate(ORDERS):
            tiles[piece] //= 2
            own = jnp.where(core == 0, place[orders[0][step]], place[orders[1][step]])
            other = joined(kept[piece], arrived[piece], (1 - own) * tiles[piece], tiles[piece])
            out = packed(other, level)
            sent.append(flipped(out, orders[0][step], orders[1][step]))
            k, m, _ = lax.optimization_barrier((kept[piece], arrived[piece], out))
            left.append(joined(k, m, own * tiles[piece], tiles[piece]))
        kept, arrived = left, sent
        level = risen(level, arrived)

    last = [packed(joined(k, m, 0, n), level) for k, m, n in zip(kept, arrived, tiles)]
    mine = jnp.concatenate([last[0][:-1], last[1]], axis=0)
    theirs = flipped(mine, Z1, Z1)
    near_place = jnp.where(core == 0, 2 * y + 1 - z0, 2 * (1 - y) + z0)
    far_place = jnp.where(core == 0, 2 * (1 - y) + z0, 2 * y + 1 - z0)
    places = jnp.stack([2 * y + z0, near_place, far_place, 2 * (1 - y) + 1 - z0]).astype(jnp.int32)
    terms = [m[:-1].astype(jnp.float32) * jnp.exp2(exponent_in(m) - 14.0) for m in (mine, theirs)]
    own = (terms[0] + terms[1]).astype(jnp.bfloat16).reshape(-1, virtuals)
    block = sum(sizes)

    def place_of(x, core, z1, z0, y):
        return (x * 2 + core) * 8 + z1 * 4 + z0 * 2 + y

    corners = [(a, b, c) for a in range(2) for b in range(2) for c in range(2)]
    over_x = [(place_of(a, b, a, b, c), place_of(1 - a, b, a, b, c)) for a, b, c in corners]
    over_x += [(place_of(a, b, a, 1 - b, c), place_of(1 - a, 1 - b, a, b, c)) for a, b, c in corners]
    over_z = [(place_of(a, b, a, 1 - b, c), place_of(a, 1 - b, a, b, c)) for a, b, c in corners]
    near = flipped(own, Z0, Y)
    from_x = lax.ppermute(own, AXES, over_x)
    from_z = lax.ppermute(own, AXES, over_z)
    partial = naf_first(sizes, places, own, naf_vectors)
    near, partial = lax.optimization_barrier((near, partial))
    pair = jnp.concatenate([own, near], axis=0)
    far = flipped(pair, Y, Z0)
    from_x, from_z, _ = lax.optimization_barrier((from_x, from_z, pair))

    part = jnp.where(x == z1, jnp.where(core == z0, own, from_z), from_x)
    other_part = flipped(part, (1, 0), (1, 0))
    halves = jnp.where(core == 0, part, other_part), jnp.where(core == 0, other_part, part)
    cuts = (0, sizes[0]), (sizes[0], block)
    columns = jnp.concatenate([half[a:b] for a, b in cuts for half in halves], axis=0)

    gram, ahead = gram_first(sizes, places, own, near, columns, naf_vectors)
    far, gram = lax.optimization_barrier((far, gram))
    partial = naf_rest(near, far, ahead, partial)
    partial = partial.reshape(4, virtuals // 4, -1)
    share = lambda flip: lax.dynamic_index_in_dim(partial, row_index ^ flip, 0, keepdims=False)
    parts = [flipped(share(flip), (flip, 0), (flip, 0)) for flip in (3, 2, 1)]
    gram = gram_rest(sizes, places, far, columns, gram)
    parts, gram = lax.optimization_barrier((parts, gram))
    naf_ints = share(0) + parts[0] + parts[1] + parts[2]
    return gram, naf_ints


def solution(mesh):
    in_specs = (P(("row", "col"), None), P(("row", "col"), None), P("row", "col"))
    out_specs = (P("row", "col"), P("row", "col"))
    plan = shards_4x8 if (mesh.shape["row"], mesh.shape["col"]) == (4, 8) else shards
    return jax.shard_map(plan, mesh=mesh, in_specs=in_specs, out_specs=out_specs, check_vma=False)
```

```python
import functools

import jax
import jax.numpy as jnp
from jax import lax
from jax.experimental import pallas as pl
from jax.experimental.pallas import tpu as pltpu
from jax.sharding import PartitionSpec as P

AXES = ("row", "col")
TILE = 16
SLOTS = 3
VMEM_LIMIT = 11 * 2**20


def contract_first(lhs, rhs):
    return lax.dot_general(lhs, rhs, (((0,), (0,)), ((), ())), preferred_element_type=jnp.float32)


def contract_second(lhs, rhs):
    return lax.dot_general(lhs, rhs, (((1,), (1,)), ((), ())), preferred_element_type=jnp.float32)


def shards(ao_ints, vir_coef, naf_vectors):
    n_row = lax.axis_size("row")
    n_col = lax.axis_size("col")
    virtuals = vir_coef.shape[1]
    aux_total = ao_ints.shape[1]
    row_width = aux_total // n_row
    col_width = aux_total // n_col
    row_index = lax.axis_index("row")
    col_index = lax.axis_index("col")
    owned_rows = lax.psum_scatter(
        contract_first(ao_ints, vir_coef), ("row", "col"), scatter_dimension=0, tiled=True
    ).astype(jnp.bfloat16)
    gathered = lax.all_gather(owned_rows, ("row", "col"), axis=0, tiled=True)
    panel_rows = lax.dynamic_slice_in_dim(gathered, row_index * row_width, row_width, 0)
    panel_cols = lax.dynamic_slice_in_dim(gathered, col_index * col_width, col_width, 0)
    tile_sum = contract_second(panel_rows, panel_cols)
    projection = contract_first(panel_rows, naf_vectors)
    naf_ints = lax.psum_scatter(projection, "row", scatter_dimension=0, tiled=True)
    return (tile_sum * (1.0 / virtuals), naf_ints)


X, Y, Z0, Z1 = (2, 0), (0, 1), (0, 2), (0, 4)
ORDERS = (((Y, Z0, X), (X, Y, Z0)), ((Z0, X, Y), (Z0, X, Y)))


def flipped(value, on_core0, on_core1):
    pairs = []
    for r in range(4):
        over_row, over_col = on_core1 if r % 2 else on_core0
        pairs += [(r * 8 + c, (r ^ over_row) * 8 + (c ^ over_col)) for c in range(8)]
    return lax.ppermute(value, AXES, pairs)


def half_blocks(sizes, bits, vir, ao):
    x, core = pl.program_id(0), bits[0]
    acc = contract_first(ao[...], vir[...])
    half = acc.shape[0] // 2
    blocks = []
    for y in range(2):
        start = y * half
        for piece, rows in enumerate(sizes):
            for z0 in range(2):
                value = acc[start : start + rows].reshape(rows // TILE, TILE, acc.shape[1])
                blocks.append((piece, place_in(piece, core, x, y, z0) * (rows // TILE), value))
                start += rows
    return blocks, jnp.max(jnp.max(jnp.abs(acc), axis=0, keepdims=True), axis=1, keepdims=True)


def place_in(piece, core, x, y, z0):
    bits = {X: x, Y: y, Z0: z0}
    on_core0, on_core1 = (sum(bits[d] * 2 ** (2 - n) for n, d in enumerate(order)) for order in ORDERS[piece])
    return jnp.where(core == 0, on_core0, on_core1)


def half_first_kernel(sizes, bits, vir, ao, *refs):
    *pieces, bound = refs
    blocks, largest = half_blocks(sizes, bits, vir, ao)

    @pl.when(pl.program_id(0) == 0)
    def _():
        bound[...] = jnp.broadcast_to(largest, bound.shape)
        for piece, at, value in blocks:
            pieces[piece][pl.ds(at, value.shape[0])] = value

    @pl.when(pl.program_id(0) == 1)
    def _():
        exponent = exponent_of(jnp.maximum(bound[...], largest))
        scale = jnp.exp2(14.0 - exponent)[None, :1]
        for piece, at, value in blocks:
            out, tiles = pieces[piece], value.shape[0]
            out[pl.ds(at, tiles)] = value * scale
            before = at - place_in(piece, bits[0], 1, 0, 0) * tiles
            earlier = out[pl.ds(before, tiles)]
            out[pl.ds(before, tiles)] = earlier * scale
        for out in pieces:
            out[out.shape[0] - 1] = jnp.concatenate([exponent, exponent], axis=0)


def half_rest_kernel(sizes, bits, vir, ao, *refs):
    *pieces, bound = refs
    blocks, largest = half_blocks(sizes, bits, vir, ao)
    for piece, at, value in blocks:
        pieces[piece][pl.ds(at, value.shape[0])] = value

    @pl.when(pl.program_id(0) == 0)
    def _():
        bound[...] = jnp.broadcast_to(largest, bound.shape)
        for out in pieces:
            out[out.shape[0] - 1] = jnp.zeros(out.shape[1:], jnp.float32)

    @pl.when(pl.program_id(0) == 1)
    def _():
        bound[...] = exponent_of(jnp.maximum(bound[...], largest))


def half_pieces(ao_ints, vir_coef, core, sizes):
    naos, aux = ao_ints.shape
    virtuals = vir_coef.shape[1]
    panel = aux // 4
    shapes = [pltpu.VMEM((8 * s // TILE + 1, TILE, virtuals), jnp.float32) for s in sizes]
    bound = pltpu.VMEM((8, virtuals), jnp.float32)
    in_vmem = pl.BlockSpec(memory_space=pltpu.VMEM)
    cost = pl.CostEstimate(flops=naos * aux * virtuals, bytes_accessed=naos * aux + 2 * aux * virtuals, transcendentals=0)
    limit = pltpu.CompilerParams(vmem_limit_bytes=5 * 2**20)
    source = pltpu.with_memory_space_constraint(ao_ints, pltpu.HBM)
    away = pl.pallas_call(
        functools.partial(half_first_kernel, sizes),
        grid_spec=pltpu.PrefetchScalarGridSpec(
            num_scalar_prefetch=1,
            grid=(2,),
            in_specs=[
                pl.BlockSpec((naos, virtuals), lambda i, b: (0, 0)),
                pl.BlockSpec((naos, panel), lambda i, b: (0, 2 * i + b[0])),
            ],
            out_specs=[in_vmem] * len(shapes),
            scratch_shapes=[bound],
        ),
        out_shape=shapes,
        compiler_params=limit,
        cost_estimate=cost,
    )((1 - core).reshape(1).astype(jnp.int32), pltpu.with_memory_space_constraint(vir_coef, pltpu.HBM), source)
    def rest():
        return pl.pallas_call(
            functools.partial(half_rest_kernel, sizes),
            grid_spec=pltpu.PrefetchScalarGridSpec(
                num_scalar_prefetch=1,
                grid=(2,),
                in_specs=[
                    pl.BlockSpec((naos, virtuals), lambda i, b: (0, 0)),
                    pl.BlockSpec((naos, panel), lambda i, b: (0, 2 * i + b[0])),
                ],
                out_specs=[in_vmem] * (len(shapes) + 1),
            ),
            out_shape=shapes + [bound],
            compiler_params=limit,
            cost_estimate=cost,
        )(core.reshape(1).astype(jnp.int32), pltpu.with_memory_space_constraint(vir_coef, pltpu.HBM), source)

    return away, rest


def exponent_of(bound):
    return jnp.ceil(jnp.log2(jnp.maximum(bound, 1e-30))) + 1.0


def packed(value, exponent):
    head = lax.broadcasted_iota(jnp.int32, value.shape, 0) == value.shape[0] - 1
    return jnp.where(head, exponent, value * jnp.exp2(14.0 - exponent)).astype(jnp.float16)


def exponent_in(message):
    return message[-1, :1].astype(jnp.float32)


def risen(level, messages):
    for message in messages:
        level = jnp.maximum(level, exponent_in(message))
    return level + 1.0


def joined(kept, message, start, tiles):
    mine = lax.dynamic_slice_in_dim(kept, start, tiles + 1, 0)
    theirs = lax.dynamic_slice_in_dim(message, start, tiles + 1, 0).astype(jnp.float32)
    return mine + theirs * jnp.exp2(exponent_in(message) - 14.0)


def row_start(place, rows, piece, sizes):
    half = 2 * sum(sizes)
    return pl.multiple_of(place // 2 * half + 2 * sum(sizes[:piece]) + place % 2 * rows, TILE)


def blocks_of(sizes, places, array, first, count):
    blocks, at = [], 0
    for n in range(count):
        for piece, rows in enumerate(sizes):
            blocks.append((array, at, rows, row_start(places[first + n], rows, piece, sizes)))
            at += rows
    return blocks


def steps_of(sizes):
    cuts = []
    for rows in sizes:
        count = max(1, round(3 * rows / sum(sizes)))
        edges = [rows * n // count // TILE * TILE for n in range(count)] + [rows]
        cuts.append(tuple(zip(edges[:-1], edges[1:])))
    return cuts


def step_rows(sizes):
    return max(b - a for cuts in steps_of(sizes) for a, b in cuts)


def gram_steps(sizes, scale, blocks, cols, out, buffers, sems):
    copies = []
    cuts = steps_of(sizes)
    for ref, at, height, start in blocks:
        for a, b in cuts[sizes.index(height)]:
            n = len(copies)
            if n >= SLOTS:
                copies[n - SLOTS].wait()
            slot = n % SLOTS
            buffers[slot, : b - a] = contract_second(ref[at + a : at + b], cols[...]) * scale
            where = pl.ds(pl.multiple_of(start + a, TILE), b - a)
            copies.append(pltpu.make_async_copy(buffers.at[slot, pl.ds(0, b - a)], out.at[where, :], sems.at[slot]))
            copies[n].start()
    for copy in copies[-SLOTS:]:
        copy.wait()


def gram_first_kernel(sizes, scale, places, own, near, cols, out, buffers, sems):
    blocks = blocks_of(sizes, places, own, 0, 1) + blocks_of(sizes, places, near, 1, 1)
    gram_steps(sizes, scale, blocks, cols, out, buffers, sems)


def gram_rest_kernel(sizes, scale, places, far, cols, begun, out, buffers, sems):
    gram_steps(sizes, scale, blocks_of(sizes, places, far, 2, 2), cols, out, buffers, sems)


def gram_first(sizes, places, own, near, cols):
    in_vmem = pl.BlockSpec(memory_space=pltpu.VMEM)
    block, virtuals = own.shape
    return pl.pallas_call(
        functools.partial(gram_first_kernel, sizes, 1.0 / virtuals),
        grid_spec=pltpu.PrefetchScalarGridSpec(
            num_scalar_prefetch=1,
            grid=(),
            in_specs=[in_vmem] * 3,
            out_specs=pl.BlockSpec(memory_space=pl.ANY),
            scratch_shapes=[pltpu.VMEM((SLOTS, step_rows(sizes), 2 * block), jnp.float32), pltpu.SemaphoreType.DMA((SLOTS,))],
        ),
        out_shape=jax.ShapeDtypeStruct((4 * block, 2 * block), jnp.float32),
        compiler_params=pltpu.CompilerParams(vmem_limit_bytes=VMEM_LIMIT),
        cost_estimate=pl.CostEstimate(flops=8 * block * block * virtuals, bytes_accessed=16 * block * block, transcendentals=0),
    )(places, own, near, cols)


def gram_rest(sizes, places, far, cols, begun):
    in_vmem = pl.BlockSpec(memory_space=pltpu.VMEM)
    in_hbm = pl.BlockSpec(memory_space=pl.ANY)
    block, virtuals = far.shape[0] // 2, far.shape[1]
    return pl.pallas_call(
        functools.partial(gram_rest_kernel, sizes, 1.0 / virtuals),
        grid_spec=pltpu.PrefetchScalarGridSpec(
            num_scalar_prefetch=1,
            grid=(),
            in_specs=[in_vmem, in_vmem, in_hbm],
            out_specs=in_hbm,
            scratch_shapes=[pltpu.VMEM((SLOTS, step_rows(sizes), 2 * block), jnp.float32), pltpu.SemaphoreType.DMA((SLOTS,))],
        ),
        out_shape=jax.ShapeDtypeStruct((4 * block, 2 * block), jnp.float32),
        input_output_aliases={3: 0},
        compiler_params=pltpu.CompilerParams(vmem_limit_bytes=VMEM_LIMIT),
        cost_estimate=pl.CostEstimate(flops=8 * block * block * virtuals, bytes_accessed=16 * block * block, transcendentals=0),
    )(places, far, cols, begun)


def naf_kernel(sizes, places, own, near, far, naf, out, panel):
    blocks = blocks_of(sizes, places, own, 0, 1) + blocks_of(sizes, places, near, 1, 1)
    for ref, at, rows, row in blocks + blocks_of(sizes, places, far, 2, 2):
        panel[pl.ds(row, rows), :] = ref[at : at + rows]
    out[...] = contract_first(panel[...], naf[...])


def project(sizes, places, own, near, far, naf_vectors):
    virtuals = own.shape[1]
    rows, nnaf = naf_vectors.shape
    in_vmem = pl.BlockSpec(memory_space=pltpu.VMEM)
    return pl.pallas_call(
        functools.partial(naf_kernel, sizes),
        grid_spec=pltpu.PrefetchScalarGridSpec(
            num_scalar_prefetch=1,
            grid=(),
            in_specs=[in_vmem] * 4,
            out_specs=in_vmem,
            scratch_shapes=[pltpu.VMEM((rows, virtuals), jnp.bfloat16)],
        ),
        out_shape=pltpu.VMEM((virtuals, nnaf), jnp.float32),
        compiler_params=pltpu.CompilerParams(vmem_limit_bytes=10 * 2**20),
        cost_estimate=pl.CostEstimate(flops=2 * rows * nnaf * virtuals, bytes_accessed=2 * rows * nnaf, transcendentals=0),
    )(places, own, near, far, naf_vectors)


def shards_4x8(ao_ints, vir_coef, naf_vectors):
    virtuals = vir_coef.shape[1]
    row_index = lax.axis_index("row")
    col_index = lax.axis_index("col")
    core, x = row_index % 2, row_index // 2
    y, z0, z1 = col_index % 2, col_index // 2 % 2, col_index // 4
    place = {X: x, Y: y, Z0: z0}
    half = ao_ints.shape[1] // 16
    sizes = (592 * half // 960 // TILE * TILE,)
    sizes += (half - sizes[0],)

    away, kept_pieces = half_pieces(ao_ints, vir_coef, core, sizes)
    arrived = [flipped(p.astype(jnp.float16), (1, 0), (1, 0)) for p in away[::-1]][::-1]
    *kept, exponent = kept_pieces()
    exponent = exponent[:1]

    level = risen(exponent, arrived)
    tiles = [8 * s // TILE for s in sizes]
    for step in range(3):
        sent, left = [], []
        for piece, orders in enumerate(ORDERS):
            tiles[piece] //= 2
            own = jnp.where(core == 0, place[orders[0][step]], place[orders[1][step]])
            other = joined(kept[piece], arrived[piece], (1 - own) * tiles[piece], tiles[piece])
            out = packed(other, level)
            if piece == 0:
                kept[1], arrived[1], out = lax.optimization_barrier((kept[1], arrived[1], out))
            sent.append(flipped(out, orders[0][step], orders[1][step]))
            k, m, _ = lax.optimization_barrier((kept[piece], arrived[piece], out))
            left.append(joined(k, m, own * tiles[piece], tiles[piece]))
        kept, arrived = left, sent
        level = risen(level, arrived)

    last = [packed(joined(k, m, 0, n), level) for k, m, n in zip(kept, arrived, tiles)]
    mine = jnp.concatenate([last[0][:-1], last[1]], axis=0)
    theirs = flipped(mine, Z1, Z1)
    near_place = jnp.where(core == 0, 2 * y + 1 - z0, 2 * (1 - y) + z0)
    far_place = jnp.where(core == 0, 2 * (1 - y) + z0, 2 * y + 1 - z0)
    places = jnp.stack([2 * y + z0, near_place, far_place, 2 * (1 - y) + 1 - z0]).astype(jnp.int32)
    terms = [m[:-1].astype(jnp.float32) * jnp.exp2(exponent_in(m) - 14.0) for m in (mine, theirs)]
    own = (terms[0] + terms[1]).astype(jnp.bfloat16).reshape(-1, virtuals)
    block = sum(sizes)

    def place_of(x, core, z1, z0, y):
        return (x * 2 + core) * 8 + z1 * 4 + z0 * 2 + y

    corners = [(a, b, c) for a in range(2) for b in range(2) for c in range(2)]
    over_x = [(place_of(a, b, a, b, c), place_of(1 - a, b, a, b, c)) for a, b, c in corners]
    over_x += [(place_of(a, b, a, 1 - b, c), place_of(1 - a, 1 - b, a, b, c)) for a, b, c in corners]
    over_z = [(place_of(a, b, a, 1 - b, c), place_of(a, 1 - b, a, b, c)) for a, b, c in corners]
    near = flipped(own, Z0, Y)
    from_x = lax.ppermute(own, AXES, over_x)
    from_z = lax.ppermute(own, AXES, over_z)
    pair = jnp.concatenate([own, near], axis=0)
    far = flipped(pair, Y, Z0)
    from_x, from_z, _ = lax.optimization_barrier((from_x, from_z, pair))

    part = jnp.where(x == z1, jnp.where(core == z0, own, from_z), from_x)
    other_part = flipped(part, (1, 0), (1, 0))
    halves = jnp.where(core == 0, part, other_part), jnp.where(core == 0, other_part, part)
    cuts = (0, sizes[0]), (sizes[0], block)
    columns = jnp.concatenate([half[a:b] for a, b in cuts for half in halves], axis=0)

    gram = gram_first(sizes, places, own, near, columns)
    far, gram = lax.optimization_barrier((far, gram))
    partial = project(sizes, places, own, near, far, naf_vectors)
    partial = partial.reshape(4, virtuals // 4, -1)
    share = lambda flip: lax.dynamic_index_in_dim(partial, row_index ^ flip, 0, keepdims=False)
    parts = [flipped(share(flip), (flip, 0), (flip, 0)) for flip in (3, 2, 1)]
    gram = gram_rest(sizes, places, far, columns, gram)
    parts, gram = lax.optimization_barrier((parts, gram))
    naf_ints = share(0) + parts[0] + parts[1] + parts[2]
    return gram, naf_ints


def solution(mesh):
    in_specs = (P(("row", "col"), None), P(("row", "col"), None), P("row", "col"))
    out_specs = (P("row", "col"), P("row", "col"))
    plan = shards_4x8 if (mesh.shape["row"], mesh.shape["col"]) == (4, 8) else shards
    return jax.shard_map(plan, mesh=mesh, in_specs=in_specs, out_specs=out_specs, check_vma=False)
```

```python
import functools

import jax
import jax.numpy as jnp
from jax import lax
from jax.experimental import pallas as pl
from jax.experimental.pallas import tpu as pltpu
from jax.sharding import PartitionSpec as P

AXES = ("row", "col")
TILE = 16
SLOTS = 3
VMEM_LIMIT = 11 * 2**20


def contract_first(lhs, rhs):
    return lax.dot_general(lhs, rhs, (((0,), (0,)), ((), ())), preferred_element_type=jnp.float32)


def contract_second(lhs, rhs):
    return lax.dot_general(lhs, rhs, (((1,), (1,)), ((), ())), preferred_element_type=jnp.float32)


def shards(ao_ints, vir_coef, naf_vectors):
    n_row = lax.axis_size("row")
    n_col = lax.axis_size("col")
    virtuals = vir_coef.shape[1]
    aux_total = ao_ints.shape[1]
    row_width = aux_total // n_row
    col_width = aux_total // n_col
    row_index = lax.axis_index("row")
    col_index = lax.axis_index("col")
    owned_rows = lax.psum_scatter(
        contract_first(ao_ints, vir_coef), ("row", "col"), scatter_dimension=0, tiled=True
    ).astype(jnp.bfloat16)
    gathered = lax.all_gather(owned_rows, ("row", "col"), axis=0, tiled=True)
    panel_rows = lax.dynamic_slice_in_dim(gathered, row_index * row_width, row_width, 0)
    panel_cols = lax.dynamic_slice_in_dim(gathered, col_index * col_width, col_width, 0)
    tile_sum = contract_second(panel_rows, panel_cols)
    projection = contract_first(panel_rows, naf_vectors)
    naf_ints = lax.psum_scatter(projection, "row", scatter_dimension=0, tiled=True)
    return (tile_sum * (1.0 / virtuals), naf_ints)


X, Y, Z0, Z1 = (2, 0), (0, 1), (0, 2), (0, 4)
ORDERS = (((Y, Z0, X), (X, Y, Z0)), ((Z0, X, Y), (Z0, X, Y)))


def flipped(value, on_core0, on_core1):
    pairs = []
    for r in range(4):
        over_row, over_col = on_core1 if r % 2 else on_core0
        pairs += [(r * 8 + c, (r ^ over_row) * 8 + (c ^ over_col)) for c in range(8)]
    return lax.ppermute(value, AXES, pairs)


def half_blocks(sizes, bits, vir, ao):
    x, core = pl.program_id(0), bits[0]
    acc = contract_first(ao[...], vir[...])
    half = acc.shape[0] // 2
    blocks = []
    for y in range(2):
        start = y * half
        for piece, rows in enumerate(sizes):
            for z0 in range(2):
                value = acc[start : start + rows].reshape(rows // TILE, TILE, acc.shape[1])
                blocks.append((piece, place_in(piece, core, x, y, z0) * (rows // TILE), value))
                start += rows
    return blocks, jnp.max(jnp.max(jnp.abs(acc), axis=0, keepdims=True), axis=1, keepdims=True)


def place_in(piece, core, x, y, z0):
    bits = {X: x, Y: y, Z0: z0}
    on_core0, on_core1 = (sum(bits[d] * 2 ** (2 - n) for n, d in enumerate(order)) for order in ORDERS[piece])
    return jnp.where(core == 0, on_core0, on_core1)


def half_first_kernel(sizes, bits, vir, ao, *refs):
    *pieces, bound = refs
    blocks, largest = half_blocks(sizes, bits, vir, ao)

    @pl.when(pl.program_id(0) == 0)
    def _():
        bound[...] = jnp.broadcast_to(largest, bound.shape)
        for piece, at, value in blocks:
            pieces[piece][pl.ds(at, value.shape[0])] = value

    @pl.when(pl.program_id(0) == 1)
    def _():
        exponent = exponent_of(jnp.maximum(bound[...], largest))
        scale = jnp.exp2(14.0 - exponent)[None, :1]
        for piece, at, value in blocks:
            out, tiles = pieces[piece], value.shape[0]
            out[pl.ds(at, tiles)] = value * scale
            before = at - place_in(piece, bits[0], 1, 0, 0) * tiles
            earlier = out[pl.ds(before, tiles)]
            out[pl.ds(before, tiles)] = earlier * scale
        for out in pieces:
            out[out.shape[0] - 1] = jnp.concatenate([exponent, exponent], axis=0)


def half_rest_kernel(sizes, bits, vir, ao, *refs):
    *pieces, bound = refs
    blocks, largest = half_blocks(sizes, bits, vir, ao)
    for piece, at, value in blocks:
        pieces[piece][pl.ds(at, value.shape[0])] = value

    @pl.when(pl.program_id(0) == 0)
    def _():
        bound[...] = jnp.broadcast_to(largest, bound.shape)
        for out in pieces:
            out[out.shape[0] - 1] = jnp.zeros(out.shape[1:], jnp.float32)

    @pl.when(pl.program_id(0) == 1)
    def _():
        bound[...] = exponent_of(jnp.maximum(bound[...], largest))


def half_pieces(ao_ints, vir_coef, core, sizes):
    naos, aux = ao_ints.shape
    virtuals = vir_coef.shape[1]
    panel = aux // 4
    shapes = [pltpu.VMEM((8 * s // TILE + 1, TILE, virtuals), jnp.float32) for s in sizes]
    bound = pltpu.VMEM((8, virtuals), jnp.float32)
    in_vmem = pl.BlockSpec(memory_space=pltpu.VMEM)
    cost = pl.CostEstimate(flops=naos * aux * virtuals, bytes_accessed=naos * aux + 2 * aux * virtuals, transcendentals=0)
    limit = pltpu.CompilerParams(vmem_limit_bytes=5 * 2**20)
    source = pltpu.with_memory_space_constraint(ao_ints, pltpu.HBM)
    away = pl.pallas_call(
        functools.partial(half_first_kernel, sizes),
        grid_spec=pltpu.PrefetchScalarGridSpec(
            num_scalar_prefetch=1,
            grid=(2,),
            in_specs=[
                pl.BlockSpec((naos, virtuals), lambda i, b: (0, 0)),
                pl.BlockSpec((naos, panel), lambda i, b: (0, 2 * i + b[0])),
            ],
            out_specs=[in_vmem] * len(shapes),
            scratch_shapes=[bound],
        ),
        out_shape=shapes,
        compiler_params=limit,
        cost_estimate=cost,
    )((1 - core).reshape(1).astype(jnp.int32), pltpu.with_memory_space_constraint(vir_coef, pltpu.HBM), source)
    def rest():
        return pl.pallas_call(
            functools.partial(half_rest_kernel, sizes),
            grid_spec=pltpu.PrefetchScalarGridSpec(
                num_scalar_prefetch=1,
                grid=(2,),
                in_specs=[
                    pl.BlockSpec((naos, virtuals), lambda i, b: (0, 0)),
                    pl.BlockSpec((naos, panel), lambda i, b: (0, 2 * i + b[0])),
                ],
                out_specs=[in_vmem] * (len(shapes) + 1),
            ),
            out_shape=shapes + [bound],
            compiler_params=limit,
            cost_estimate=cost,
        )(core.reshape(1).astype(jnp.int32), pltpu.with_memory_space_constraint(vir_coef, pltpu.HBM), source)

    return away, rest


def exponent_of(bound):
    return jnp.ceil(jnp.log2(jnp.maximum(bound, 1e-30))) + 1.0


def packed(value, exponent):
    head = lax.broadcasted_iota(jnp.int32, value.shape, 0) == value.shape[0] - 1
    return jnp.where(head, exponent, value * jnp.exp2(14.0 - exponent)).astype(jnp.float16)


def exponent_in(message):
    return message[-1, :1].astype(jnp.float32)


def risen(level, messages):
    for message in messages:
        level = jnp.maximum(level, exponent_in(message))
    return level + 1.0


def joined(kept, message, start, tiles):
    mine = lax.dynamic_slice_in_dim(kept, start, tiles + 1, 0)
    theirs = lax.dynamic_slice_in_dim(message, start, tiles + 1, 0).astype(jnp.float32)
    return mine + theirs * jnp.exp2(exponent_in(message) - 14.0)


def row_start(place, rows, piece, sizes):
    half = 2 * sum(sizes)
    return pl.multiple_of(place // 2 * half + 2 * sum(sizes[:piece]) + place % 2 * rows, TILE)


def blocks_of(sizes, places, array, first, count):
    blocks, at = [], 0
    for n in range(count):
        for piece, rows in enumerate(sizes):
            blocks.append((array, at, rows, row_start(places[first + n], rows, piece, sizes)))
            at += rows
    return blocks


def steps_of(sizes):
    cuts = []
    for rows in sizes:
        count = max(1, round(3 * rows / sum(sizes)))
        edges = [rows * n // count // TILE * TILE for n in range(count)] + [rows]
        cuts.append(tuple(zip(edges[:-1], edges[1:])))
    return cuts


def step_rows(sizes):
    return max(b - a for cuts in steps_of(sizes) for a, b in cuts)


def gram_steps(sizes, scale, blocks, cols, out, buffers, sems):
    copies = []
    cuts = steps_of(sizes)
    for ref, at, height, start in blocks:
        for a, b in cuts[sizes.index(height)]:
            n = len(copies)
            if n >= SLOTS:
                copies[n - SLOTS].wait()
            slot = n % SLOTS
            buffers[slot, : b - a] = contract_second(ref[at + a : at + b], cols[...]) * scale
            where = pl.ds(pl.multiple_of(start + a, TILE), b - a)
            copies.append(pltpu.make_async_copy(buffers.at[slot, pl.ds(0, b - a)], out.at[where, :], sems.at[slot]))
            copies[n].start()
    for copy in copies[-SLOTS:]:
        copy.wait()


def gram_first_kernel(sizes, scale, places, pair, cols, out, buffers, sems):
    blocks = blocks_of(sizes, (places[0], places[2]), pair, 0, 2)
    gram_steps(sizes, scale, blocks, cols, out, buffers, sems)


def gram_rest_kernel(sizes, scale, places, near, far, cols, begun, out, buffers, sems):
    blocks = blocks_of(sizes, places, near, 1, 1) + blocks_of(sizes, places, far, 3, 1)
    gram_steps(sizes, scale, blocks, cols, out, buffers, sems)


def gram_first(sizes, places, pair, cols):
    in_vmem = pl.BlockSpec(memory_space=pltpu.VMEM)
    block, virtuals = pair.shape[0] // 2, pair.shape[1]
    return pl.pallas_call(
        functools.partial(gram_first_kernel, sizes, 1.0 / virtuals),
        grid_spec=pltpu.PrefetchScalarGridSpec(
            num_scalar_prefetch=1,
            grid=(),
            in_specs=[in_vmem] * 2,
            out_specs=pl.BlockSpec(memory_space=pl.ANY),
            scratch_shapes=[pltpu.VMEM((SLOTS, step_rows(sizes), 2 * block), jnp.float32), pltpu.SemaphoreType.DMA((SLOTS,))],
        ),
        out_shape=jax.ShapeDtypeStruct((4 * block, 2 * block), jnp.float32),
        compiler_params=pltpu.CompilerParams(vmem_limit_bytes=VMEM_LIMIT),
        cost_estimate=pl.CostEstimate(flops=8 * block * block * virtuals, bytes_accessed=16 * block * block, transcendentals=0),
    )(places, pair, cols)


def gram_rest(sizes, places, near, far, cols, begun):
    in_vmem = pl.BlockSpec(memory_space=pltpu.VMEM)
    in_hbm = pl.BlockSpec(memory_space=pl.ANY)
    block, virtuals = far.shape
    return pl.pallas_call(
        functools.partial(gram_rest_kernel, sizes, 1.0 / virtuals),
        grid_spec=pltpu.PrefetchScalarGridSpec(
            num_scalar_prefetch=1,
            grid=(),
            in_specs=[in_vmem, in_vmem, in_vmem, in_hbm],
            out_specs=in_hbm,
            scratch_shapes=[pltpu.VMEM((SLOTS, step_rows(sizes), 2 * block), jnp.float32), pltpu.SemaphoreType.DMA((SLOTS,))],
        ),
        out_shape=jax.ShapeDtypeStruct((4 * block, 2 * block), jnp.float32),
        input_output_aliases={4: 0},
        compiler_params=pltpu.CompilerParams(vmem_limit_bytes=VMEM_LIMIT),
        cost_estimate=pl.CostEstimate(flops=8 * block * block * virtuals, bytes_accessed=16 * block * block, transcendentals=0),
    )(places, near, far, cols, begun)


def naf_kernel(sizes, places, own, near, side, far, naf, out, panel):
    for n, block in enumerate((own, near, side, far)):
        for ref, at, rows, row in blocks_of(sizes, places, block, n, 1):
            panel[pl.ds(row, rows), :] = ref[at : at + rows]
    out[...] = contract_first(panel[...], naf[...])


def project(sizes, places, own, near, side, far, naf_vectors):
    virtuals = own.shape[1]
    rows, nnaf = naf_vectors.shape
    in_vmem = pl.BlockSpec(memory_space=pltpu.VMEM)
    return pl.pallas_call(
        functools.partial(naf_kernel, sizes),
        grid_spec=pltpu.PrefetchScalarGridSpec(
            num_scalar_prefetch=1,
            grid=(),
            in_specs=[in_vmem] * 5,
            out_specs=in_vmem,
            scratch_shapes=[pltpu.VMEM((rows, virtuals), jnp.bfloat16)],
        ),
        out_shape=pltpu.VMEM((virtuals, nnaf), jnp.float32),
        compiler_params=pltpu.CompilerParams(vmem_limit_bytes=10 * 2**20),
        cost_estimate=pl.CostEstimate(flops=2 * rows * nnaf * virtuals, bytes_accessed=2 * rows * nnaf, transcendentals=0),
    )(places, own, near, side, far, naf_vectors)


def shards_4x8(ao_ints, vir_coef, naf_vectors):
    virtuals = vir_coef.shape[1]
    row_index = lax.axis_index("row")
    col_index = lax.axis_index("col")
    core, x = row_index % 2, row_index // 2
    y, z0, z1 = col_index % 2, col_index // 2 % 2, col_index // 4
    place = {X: x, Y: y, Z0: z0}
    half = ao_ints.shape[1] // 16
    sizes = (592 * half // 960 // TILE * TILE,)
    sizes += (half - sizes[0],)

    away, kept_pieces = half_pieces(ao_ints, vir_coef, core, sizes)
    arrived = [flipped(p.astype(jnp.float16), (1, 0), (1, 0)) for p in away[::-1]][::-1]
    *kept, exponent = kept_pieces()
    exponent = exponent[:1]

    level = risen(exponent, arrived)
    tiles = [8 * s // TILE for s in sizes]
    for step in range(3):
        sent, left = [], []
        for piece, orders in enumerate(ORDERS):
            tiles[piece] //= 2
            own = jnp.where(core == 0, place[orders[0][step]], place[orders[1][step]])
            other = joined(kept[piece], arrived[piece], (1 - own) * tiles[piece], tiles[piece])
            out = packed(other, level)
            if piece == 0:
                kept[1], arrived[1], out = lax.optimization_barrier((kept[1], arrived[1], out))
            sent.append(flipped(out, orders[0][step], orders[1][step]))
            k, m, _ = lax.optimization_barrier((kept[piece], arrived[piece], out))
            left.append(joined(k, m, own * tiles[piece], tiles[piece]))
        kept, arrived = left, sent
        level = risen(level, arrived)

    last = [packed(joined(k, m, 0, n), level) for k, m, n in zip(kept, arrived, tiles)]
    mine = jnp.concatenate([last[0][:-1], last[1]], axis=0)
    theirs = flipped(mine, Z1, Z1)
    places = jnp.stack([2 * (i ^ y) + (j ^ z0) for i in range(2) for j in range(2)]).astype(jnp.int32)
    terms = [m[:-1].astype(jnp.float32) * jnp.exp2(exponent_in(m) - 14.0) for m in (mine, theirs)]
    own = (terms[0] + terms[1]).astype(jnp.bfloat16).reshape(-1, virtuals)
    block = sum(sizes)

    def place_of(x, core, z1, z0, y):
        return (x * 2 + core) * 8 + z1 * 4 + z0 * 2 + y

    corners = [(a, b, c) for a in range(2) for b in range(2) for c in range(2)]
    over_x = [(place_of(a, b, a, b, c), place_of(1 - a, b, a, b, c)) for a, b, c in corners]
    over_x += [(place_of(a, b, a, 1 - b, c), place_of(1 - a, 1 - b, a, b, c)) for a, b, c in corners]
    near = flipped(own, Z0, Z0)
    from_x = lax.ppermute(own, AXES, over_x)
    side = flipped(own, Y, Y)
    pair = jnp.concatenate([own, side], axis=0)
    from_x, near, pair = lax.optimization_barrier((from_x, near, pair))
    here = jnp.where(x == z1, own, from_x)
    there = jnp.where(x == z1, near, from_x)
    mine = jnp.where(z0 == 0, jnp.concatenate([here, there], axis=0), jnp.concatenate([there, here], axis=0))
    theirs = flipped(mine, (1, 0), (1, 0))
    far = flipped(near, Y, Y)
    first_mine = (core == z0) == ((z0 == 0) | (x == z1))
    second_mine = (core == z0) == ((z0 == 1) | (x == z1))
    halves = jnp.where(first_mine, mine[:block], theirs[:block]), jnp.where(second_mine, mine[block:], theirs[block:])
    cuts = (0, sizes[0]), (sizes[0], block)
    columns = jnp.concatenate([half[a:b] for a, b in cuts for half in halves], axis=0)

    gram = gram_first(sizes, places, pair, columns)
    far, gram = lax.optimization_barrier((far, gram))
    partial = project(sizes, places, own, near, pair[block:], far, naf_vectors)
    partial = partial.reshape(4, virtuals // 4, -1)
    share = lambda flip: lax.dynamic_index_in_dim(partial, row_index ^ flip, 0, keepdims=False)
    parts = [flipped(share(flip), (flip, 0), (flip, 0)) for flip in (3, 2, 1)]
    gram = gram_rest(sizes, places, near, far, columns, gram)
    parts, gram = lax.optimization_barrier((parts, gram))
    naf_ints = share(0) + parts[0] + parts[1] + parts[2]
    return gram, naf_ints


def solution(mesh):
    in_specs = (P(("row", "col"), None), P(("row", "col"), None), P("row", "col"))
    out_specs = (P("row", "col"), P("row", "col"))
    plan = shards_4x8 if (mesh.shape["row"], mesh.shape["col"]) == (4, 8) else shards
    return jax.shard_map(plan, mesh=mesh, in_specs=in_specs, out_specs=out_specs, check_vma=False)
```

```python
import functools

import jax
import jax.numpy as jnp
from jax import lax
from jax.experimental import pallas as pl
from jax.experimental.pallas import tpu as pltpu
from jax.sharding import PartitionSpec as P

AXES = ("row", "col")
TILE = 16
SLOTS = 3
VMEM_LIMIT = 11 * 2**20


def contract_first(lhs, rhs):
    return lax.dot_general(lhs, rhs, (((0,), (0,)), ((), ())), preferred_element_type=jnp.float32)


def contract_second(lhs, rhs):
    return lax.dot_general(lhs, rhs, (((1,), (1,)), ((), ())), preferred_element_type=jnp.float32)


def shards(ao_ints, vir_coef, naf_vectors):
    n_row = lax.axis_size("row")
    n_col = lax.axis_size("col")
    virtuals = vir_coef.shape[1]
    aux_total = ao_ints.shape[1]
    row_width = aux_total // n_row
    col_width = aux_total // n_col
    row_index = lax.axis_index("row")
    col_index = lax.axis_index("col")
    owned_rows = lax.psum_scatter(
        contract_first(ao_ints, vir_coef), ("row", "col"), scatter_dimension=0, tiled=True
    ).astype(jnp.bfloat16)
    gathered = lax.all_gather(owned_rows, ("row", "col"), axis=0, tiled=True)
    panel_rows = lax.dynamic_slice_in_dim(gathered, row_index * row_width, row_width, 0)
    panel_cols = lax.dynamic_slice_in_dim(gathered, col_index * col_width, col_width, 0)
    tile_sum = contract_second(panel_rows, panel_cols)
    projection = contract_first(panel_rows, naf_vectors)
    naf_ints = lax.psum_scatter(projection, "row", scatter_dimension=0, tiled=True)
    return (tile_sum * (1.0 / virtuals), naf_ints)


X, Y, Z0, Z1 = (2, 0), (0, 1), (0, 2), (0, 4)
ORDERS = (((Y, Z0, X), (X, Y, Z0)), ((Z0, X, Y), (Z0, X, Y)))


def flipped(value, on_core0, on_core1):
    pairs = []
    for r in range(4):
        over_row, over_col = on_core1 if r % 2 else on_core0
        pairs += [(r * 8 + c, (r ^ over_row) * 8 + (c ^ over_col)) for c in range(8)]
    return lax.ppermute(value, AXES, pairs)


def half_blocks(sizes, bits, vir, ao):
    x, core = pl.program_id(0), bits[0]
    acc = contract_first(ao[...], vir[...])
    half = acc.shape[0] // 2
    blocks = []
    for y in range(2):
        start = y * half
        for piece, rows in enumerate(sizes):
            for z0 in range(2):
                value = acc[start : start + rows].reshape(rows // TILE, TILE, acc.shape[1])
                blocks.append((piece, place_in(piece, core, x, y, z0) * (rows // TILE), value))
                start += rows
    return blocks, jnp.max(jnp.max(jnp.abs(acc), axis=0, keepdims=True), axis=1, keepdims=True)


def place_in(piece, core, x, y, z0):
    bits = {X: x, Y: y, Z0: z0}
    on_core0, on_core1 = (sum(bits[d] * 2 ** (2 - n) for n, d in enumerate(order)) for order in ORDERS[piece])
    return jnp.where(core == 0, on_core0, on_core1)


def half_first_kernel(sizes, bits, vir, ao, *refs):
    *pieces, bound = refs
    blocks, largest = half_blocks(sizes, bits, vir, ao)

    @pl.when(pl.program_id(0) == 0)
    def _():
        bound[...] = jnp.broadcast_to(largest, bound.shape)
        for piece, at, value in blocks:
            pieces[piece][pl.ds(at, value.shape[0])] = value

    @pl.when(pl.program_id(0) == 1)
    def _():
        exponent = exponent_of(jnp.maximum(bound[...], largest))
        scale = jnp.exp2(14.0 - exponent)[None, :1]
        for piece, at, value in blocks:
            out, tiles = pieces[piece], value.shape[0]
            out[pl.ds(at, tiles)] = value * scale
            before = at - place_in(piece, bits[0], 1, 0, 0) * tiles
            earlier = out[pl.ds(before, tiles)]
            out[pl.ds(before, tiles)] = earlier * scale
        for out in pieces:
            out[out.shape[0] - 1] = jnp.concatenate([exponent, exponent], axis=0)


def half_rest_kernel(sizes, bits, vir, ao, *refs):
    *pieces, bound = refs
    blocks, largest = half_blocks(sizes, bits, vir, ao)
    for piece, at, value in blocks:
        pieces[piece][pl.ds(at, value.shape[0])] = value

    @pl.when(pl.program_id(0) == 0)
    def _():
        bound[...] = jnp.broadcast_to(largest, bound.shape)
        for out in pieces:
            out[out.shape[0] - 1] = jnp.zeros(out.shape[1:], jnp.float32)

    @pl.when(pl.program_id(0) == 1)
    def _():
        bound[...] = exponent_of(jnp.maximum(bound[...], largest))


def half_pieces(ao_ints, vir_coef, core, sizes):
    naos, aux = ao_ints.shape
    virtuals = vir_coef.shape[1]
    panel = aux // 4
    shapes = [pltpu.VMEM((8 * s // TILE + 1, TILE, virtuals), jnp.float32) for s in sizes]
    bound = pltpu.VMEM((8, virtuals), jnp.float32)
    in_vmem = pl.BlockSpec(memory_space=pltpu.VMEM)
    cost = pl.CostEstimate(flops=naos * aux * virtuals, bytes_accessed=naos * aux + 2 * aux * virtuals, transcendentals=0)
    limit = pltpu.CompilerParams(vmem_limit_bytes=5 * 2**20)
    source = pltpu.with_memory_space_constraint(ao_ints, pltpu.HBM)
    away = pl.pallas_call(
        functools.partial(half_first_kernel, sizes),
        grid_spec=pltpu.PrefetchScalarGridSpec(
            num_scalar_prefetch=1,
            grid=(2,),
            in_specs=[
                pl.BlockSpec((naos, virtuals), lambda i, b: (0, 0)),
                pl.BlockSpec((naos, panel), lambda i, b: (0, 2 * i + b[0])),
            ],
            out_specs=[in_vmem] * len(shapes),
            scratch_shapes=[bound],
        ),
        out_shape=shapes,
        compiler_params=limit,
        cost_estimate=cost,
    )((1 - core).reshape(1).astype(jnp.int32), pltpu.with_memory_space_constraint(vir_coef, pltpu.HBM), source)
    def rest():
        return pl.pallas_call(
            functools.partial(half_rest_kernel, sizes),
            grid_spec=pltpu.PrefetchScalarGridSpec(
                num_scalar_prefetch=1,
                grid=(2,),
                in_specs=[
                    pl.BlockSpec((naos, virtuals), lambda i, b: (0, 0)),
                    pl.BlockSpec((naos, panel), lambda i, b: (0, 2 * i + b[0])),
                ],
                out_specs=[in_vmem] * (len(shapes) + 1),
            ),
            out_shape=shapes + [bound],
            compiler_params=limit,
            cost_estimate=cost,
        )(core.reshape(1).astype(jnp.int32), pltpu.with_memory_space_constraint(vir_coef, pltpu.HBM), source)

    return away, rest


def exponent_of(bound):
    return jnp.ceil(jnp.log2(jnp.maximum(bound, 1e-30))) + 1.0


def packed(value, exponent):
    head = lax.broadcasted_iota(jnp.int32, value.shape, 0) == value.shape[0] - 1
    return jnp.where(head, exponent, value * jnp.exp2(14.0 - exponent)).astype(jnp.float16)


def exponent_in(message):
    return message[-1, :1].astype(jnp.float32)


def risen(level, messages):
    for message in messages:
        level = jnp.maximum(level, exponent_in(message))
    return level + 1.0


def joined(kept, message, start, tiles):
    mine = lax.dynamic_slice_in_dim(kept, start, tiles + 1, 0)
    theirs = lax.dynamic_slice_in_dim(message, start, tiles + 1, 0).astype(jnp.float32)
    return mine + theirs * jnp.exp2(exponent_in(message) - 14.0)


def row_start(place, rows, piece, sizes):
    half = 2 * sum(sizes)
    return pl.multiple_of(place // 2 * half + 2 * sum(sizes[:piece]) + place % 2 * rows, TILE)


def blocks_of(sizes, places, array, first, count):
    blocks, at = [], 0
    for n in range(count):
        for piece, rows in enumerate(sizes):
            blocks.append((array, at, rows, row_start(places[first + n], rows, piece, sizes)))
            at += rows
    return blocks


def steps_of(sizes):
    cuts = []
    for rows in sizes:
        count = max(1, round(3 * rows / sum(sizes)))
        edges = [rows * n // count // TILE * TILE for n in range(count)] + [rows]
        cuts.append(tuple(zip(edges[:-1], edges[1:])))
    return cuts


def step_rows(sizes):
    return max(b - a for cuts in steps_of(sizes) for a, b in cuts)


def gram_steps(sizes, scale, blocks, cols, out, buffers, sems, beside=()):
    copies = []
    cuts = steps_of(sizes)
    for ref, at, height, start in blocks:
        for a, b in cuts[sizes.index(height)]:
            n = len(copies)
            if n >= SLOTS:
                copies[n - SLOTS].wait()
            slot = n % SLOTS
            buffers[slot, : b - a] = contract_second(ref[at + a : at + b], cols[...]) * scale
            where = pl.ds(pl.multiple_of(start + a, TILE), b - a)
            copies.append(pltpu.make_async_copy(buffers.at[slot, pl.ds(0, b - a)], out.at[where, :], sems.at[slot]))
            copies[n].start()
            if n < len(beside):
                beside[n]()
    for copy in copies[-SLOTS:]:
        copy.wait()


def gram_first_kernel(sizes, scale, places, pair, near, cols, naf, out, partial, ahead, buffers, rows_in, sems, naf_sems):
    blocks = blocks_of(sizes, (places[0], places[2]), pair, 0, 2)
    terms, loads, at = [], [], 0
    for ref, first, height, row in blocks + blocks_of(sizes, places, near, 1, 1):
        here = rows_in.at[pl.ds(at, height), :]
        loads.append(pltpu.make_async_copy(naf.at[pl.ds(row, height), :], here, naf_sems.at[len(loads)]))
        terms.append((ref, first, at, height))
        at += height
    for _, first, height, row in blocks_of(sizes, places, ahead, 3, 1):
        here = ahead.at[pl.ds(first, height), :]
        loads.append(pltpu.make_async_copy(naf.at[pl.ds(row, height), :], here, naf_sems.at[len(loads)]))
    for load in loads:
        load.start()

    def add(n):
        ref, first, at, height = terms[n]
        loads[n].wait()
        term = contract_first(ref[first : first + height], rows_in[at : at + height])
        partial[...] = term if n == 0 else partial[...] + term

    beside = [functools.partial(add, n) for n in range(len(terms))]
    gram_steps(sizes, scale, blocks, cols, out, buffers, sems, beside)
    for load in loads[len(terms) :]:
        load.wait()


def gram_rest_kernel(sizes, scale, places, near, far, cols, begun, out, buffers, sems):
    blocks = blocks_of(sizes, places, near, 1, 1) + blocks_of(sizes, places, far, 3, 1)
    gram_steps(sizes, scale, blocks, cols, out, buffers, sems)


def gram_first(sizes, places, pair, near, cols, naf_vectors):
    in_vmem = pl.BlockSpec(memory_space=pltpu.VMEM)
    in_hbm = pl.BlockSpec(memory_space=pl.ANY)
    block, virtuals = near.shape
    nnaf = naf_vectors.shape[1]
    return pl.pallas_call(
        functools.partial(gram_first_kernel, sizes, 1.0 / virtuals),
        grid_spec=pltpu.PrefetchScalarGridSpec(
            num_scalar_prefetch=1,
            grid=(),
            in_specs=[in_vmem] * 3 + [in_hbm],
            out_specs=[in_hbm, in_vmem, in_vmem],
            scratch_shapes=[
                pltpu.VMEM((SLOTS, step_rows(sizes), 2 * block), jnp.float32),
                pltpu.VMEM((3 * block, nnaf), jnp.bfloat16),
                pltpu.SemaphoreType.DMA((SLOTS,)),
                pltpu.SemaphoreType.DMA((8,)),
            ],
        ),
        out_shape=[
            jax.ShapeDtypeStruct((4 * block, 2 * block), jnp.float32),
            pltpu.VMEM((virtuals, nnaf), jnp.float32),
            pltpu.VMEM((block, nnaf), jnp.bfloat16),
        ],
        compiler_params=pltpu.CompilerParams(vmem_limit_bytes=18 * 2**20),
        cost_estimate=pl.CostEstimate(flops=8 * block * block * virtuals, bytes_accessed=16 * block * block, transcendentals=0),
    )(places, pair, near, cols, pltpu.with_memory_space_constraint(naf_vectors, pltpu.HBM))


def gram_rest(sizes, places, near, far, cols, begun):
    in_vmem = pl.BlockSpec(memory_space=pltpu.VMEM)
    in_hbm = pl.BlockSpec(memory_space=pl.ANY)
    block, virtuals = far.shape
    return pl.pallas_call(
        functools.partial(gram_rest_kernel, sizes, 1.0 / virtuals),
        grid_spec=pltpu.PrefetchScalarGridSpec(
            num_scalar_prefetch=1,
            grid=(),
            in_specs=[in_vmem, in_vmem, in_vmem, in_hbm],
            out_specs=in_hbm,
            scratch_shapes=[pltpu.VMEM((SLOTS, step_rows(sizes), 2 * block), jnp.float32), pltpu.SemaphoreType.DMA((SLOTS,))],
        ),
        out_shape=jax.ShapeDtypeStruct((4 * block, 2 * block), jnp.float32),
        input_output_aliases={4: 0},
        compiler_params=pltpu.CompilerParams(vmem_limit_bytes=VMEM_LIMIT),
        cost_estimate=pl.CostEstimate(flops=8 * block * block * virtuals, bytes_accessed=16 * block * block, transcendentals=0),
    )(places, near, far, cols, begun)


def naf_kernel(far, ahead, before, out):
    out[...] = before[...] + contract_first(far[...], ahead[...])


def project(far, ahead, before):
    in_vmem = pl.BlockSpec(memory_space=pltpu.VMEM)
    return pl.pallas_call(
        naf_kernel,
        in_specs=[in_vmem] * 3,
        out_specs=in_vmem,
        out_shape=pltpu.VMEM(before.shape, jnp.float32),
        compiler_params=pltpu.CompilerParams(vmem_limit_bytes=5 * 2**20),
        cost_estimate=pl.CostEstimate(flops=2 * far.shape[0] * before.size, bytes_accessed=0, transcendentals=0),
    )(far, ahead, before)


def shards_4x8(ao_ints, vir_coef, naf_vectors):
    virtuals = vir_coef.shape[1]
    row_index = lax.axis_index("row")
    col_index = lax.axis_index("col")
    core, x = row_index % 2, row_index // 2
    y, z0, z1 = col_index % 2, col_index // 2 % 2, col_index // 4
    place = {X: x, Y: y, Z0: z0}
    half = ao_ints.shape[1] // 16
    sizes = (592 * half // 960 // TILE * TILE,)
    sizes += (half - sizes[0],)

    away, kept_pieces = half_pieces(ao_ints, vir_coef, core, sizes)
    arrived = [flipped(p.astype(jnp.float16), (1, 0), (1, 0)) for p in away[::-1]][::-1]
    *kept, exponent = kept_pieces()
    exponent = exponent[:1]

    level = risen(exponent, arrived)
    tiles = [8 * s // TILE for s in sizes]
    for step in range(3):
        sent, left = [], []
        for piece, orders in enumerate(ORDERS):
            tiles[piece] //= 2
            own = jnp.where(core == 0, place[orders[0][step]], place[orders[1][step]])
            other = joined(kept[piece], arrived[piece], (1 - own) * tiles[piece], tiles[piece])
            out = packed(other, level)
            if piece == 0:
                kept[1], arrived[1], out = lax.optimization_barrier((kept[1], arrived[1], out))
            sent.append(flipped(out, orders[0][step], orders[1][step]))
            k, m, _ = lax.optimization_barrier((kept[piece], arrived[piece], out))
            left.append(joined(k, m, own * tiles[piece], tiles[piece]))
        kept, arrived = left, sent
        level = risen(level, arrived)

    last = [packed(joined(k, m, 0, n), level) for k, m, n in zip(kept, arrived, tiles)]
    mine = jnp.concatenate([last[0][:-1], last[1]], axis=0)
    theirs = flipped(mine, Z1, Z1)
    places = jnp.stack([2 * (i ^ y) + (j ^ z0) for i in range(2) for j in range(2)]).astype(jnp.int32)
    terms = [m[:-1].astype(jnp.float32) * jnp.exp2(exponent_in(m) - 14.0) for m in (mine, theirs)]
    own = (terms[0] + terms[1]).astype(jnp.bfloat16).reshape(-1, virtuals)
    block = sum(sizes)

    def place_of(x, core, z1, z0, y):
        return (x * 2 + core) * 8 + z1 * 4 + z0 * 2 + y

    corners = [(a, b, c) for a in range(2) for b in range(2) for c in range(2)]
    over_x = [(place_of(a, b, a, b, c), place_of(1 - a, b, a, b, c)) for a, b, c in corners]
    over_x += [(place_of(a, b, a, 1 - b, c), place_of(1 - a, 1 - b, a, b, c)) for a, b, c in corners]
    near = flipped(own, Z0, Z0)
    from_x = lax.ppermute(own, AXES, over_x)
    side = flipped(own, Y, Y)
    pair = jnp.concatenate([own, side], axis=0)
    from_x, near, pair = lax.optimization_barrier((from_x, near, pair))
    here = jnp.where(x == z1, own, from_x)
    there = jnp.where(x == z1, near, from_x)
    mine = jnp.where(z0 == 0, jnp.concatenate([here, there], axis=0), jnp.concatenate([there, here], axis=0))
    theirs = flipped(mine, (1, 0), (1, 0))
    far = flipped(near, Y, Y)
    first_mine = (core == z0) == ((z0 == 0) | (x == z1))
    second_mine = (core == z0) == ((z0 == 1) | (x == z1))
    halves = jnp.where(first_mine, mine[:block], theirs[:block]), jnp.where(second_mine, mine[block:], theirs[block:])
    cuts = (0, sizes[0]), (sizes[0], block)
    columns = jnp.concatenate([half[a:b] for a, b in cuts for half in halves], axis=0)

    gram, partial, ahead = gram_first(sizes, places, pair, near, columns, naf_vectors)
    far, gram = lax.optimization_barrier((far, gram))
    partial = project(far, ahead, partial)
    partial = partial.reshape(4, virtuals // 4, -1)
    share = lambda flip: lax.dynamic_index_in_dim(partial, row_index ^ flip, 0, keepdims=False)
    parts = [flipped(share(flip), (flip, 0), (flip, 0)) for flip in (3, 2, 1)]
    gram = gram_rest(sizes, places, near, far, columns, gram)
    parts, gram = lax.optimization_barrier((parts, gram))
    naf_ints = share(0) + parts[0] + parts[1] + parts[2]
    return gram, naf_ints


def solution(mesh):
    in_specs = (P(("row", "col"), None), P(("row", "col"), None), P("row", "col"))
    out_specs = (P("row", "col"), P("row", "col"))
    plan = shards_4x8 if (mesh.shape["row"], mesh.shape["col"]) == (4, 8) else shards
    return jax.shard_map(plan, mesh=mesh, in_specs=in_specs, out_specs=out_specs, check_vma=False)
```

```python
import functools

import jax
import jax.numpy as jnp
from jax import lax
from jax.experimental import pallas as pl
from jax.experimental.pallas import tpu as pltpu
from jax.sharding import PartitionSpec as P

AXES = ("row", "col")
TILE = 16
SLOTS = 3
VMEM_LIMIT = 11 * 2**20


def contract_first(lhs, rhs):
    return lax.dot_general(lhs, rhs, (((0,), (0,)), ((), ())), preferred_element_type=jnp.float32)


def contract_second(lhs, rhs):
    return lax.dot_general(lhs, rhs, (((1,), (1,)), ((), ())), preferred_element_type=jnp.float32)


def shards(ao_ints, vir_coef, naf_vectors):
    n_row = lax.axis_size("row")
    n_col = lax.axis_size("col")
    virtuals = vir_coef.shape[1]
    aux_total = ao_ints.shape[1]
    row_width = aux_total // n_row
    col_width = aux_total // n_col
    row_index = lax.axis_index("row")
    col_index = lax.axis_index("col")
    owned_rows = lax.psum_scatter(
        contract_first(ao_ints, vir_coef), ("row", "col"), scatter_dimension=0, tiled=True
    ).astype(jnp.bfloat16)
    gathered = lax.all_gather(owned_rows, ("row", "col"), axis=0, tiled=True)
    panel_rows = lax.dynamic_slice_in_dim(gathered, row_index * row_width, row_width, 0)
    panel_cols = lax.dynamic_slice_in_dim(gathered, col_index * col_width, col_width, 0)
    tile_sum = contract_second(panel_rows, panel_cols)
    projection = contract_first(panel_rows, naf_vectors)
    naf_ints = lax.psum_scatter(projection, "row", scatter_dimension=0, tiled=True)
    return (tile_sum * (1.0 / virtuals), naf_ints)


X, Y, Z0, Z1 = (2, 0), (0, 1), (0, 2), (0, 4)
ORDERS = (((Y, Z0, X), (X, Y, Z0)), ((Z0, X, Y), (Z0, X, Y)))


def flipped(value, on_core0, on_core1):
    pairs = []
    for r in range(4):
        over_row, over_col = on_core1 if r % 2 else on_core0
        pairs += [(r * 8 + c, (r ^ over_row) * 8 + (c ^ over_col)) for c in range(8)]
    return lax.ppermute(value, AXES, pairs)


def half_blocks(sizes, bits, vir, ao):
    x, core = pl.program_id(0), bits[0]
    acc = contract_first(ao[...], vir[...])
    half = acc.shape[0] // 2
    blocks = []
    for y in range(2):
        start = y * half
        for piece, rows in enumerate(sizes):
            for z0 in range(2):
                value = acc[start : start + rows].reshape(rows // TILE, TILE, acc.shape[1])
                blocks.append((piece, place_in(piece, core, x, y, z0) * (rows // TILE), value))
                start += rows
    return blocks, jnp.max(jnp.max(jnp.abs(acc), axis=0, keepdims=True), axis=1, keepdims=True)


def place_in(piece, core, x, y, z0):
    bits = {X: x, Y: y, Z0: z0}
    on_core0, on_core1 = (sum(bits[d] * 2 ** (2 - n) for n, d in enumerate(order)) for order in ORDERS[piece])
    return jnp.where(core == 0, on_core0, on_core1)


def half_first_kernel(sizes, bits, vir, ao, *refs):
    *pieces, bound = refs
    blocks, largest = half_blocks(sizes, bits, vir, ao)

    @pl.when(pl.program_id(0) == 0)
    def _():
        bound[...] = jnp.broadcast_to(largest, bound.shape)
        for piece, at, value in blocks:
            pieces[piece][pl.ds(at, value.shape[0])] = value

    @pl.when(pl.program_id(0) == 1)
    def _():
        exponent = exponent_of(jnp.maximum(bound[...], largest))
        scale = jnp.exp2(14.0 - exponent)[None, :1]
        for piece, at, value in blocks:
            out, tiles = pieces[piece], value.shape[0]
            out[pl.ds(at, tiles)] = value * scale
            before = at - place_in(piece, bits[0], 1, 0, 0) * tiles
            earlier = out[pl.ds(before, tiles)]
            out[pl.ds(before, tiles)] = earlier * scale
        for out in pieces:
            out[out.shape[0] - 1] = jnp.concatenate([exponent, exponent], axis=0)


def half_rest_kernel(sizes, bits, vir, ao, *refs):
    *pieces, bound = refs
    blocks, largest = half_blocks(sizes, bits, vir, ao)
    for piece, at, value in blocks:
        pieces[piece][pl.ds(at, value.shape[0])] = value

    @pl.when(pl.program_id(0) == 0)
    def _():
        bound[...] = jnp.broadcast_to(largest, bound.shape)
        for out in pieces:
            out[out.shape[0] - 1] = jnp.zeros(out.shape[1:], jnp.float32)

    @pl.when(pl.program_id(0) == 1)
    def _():
        bound[...] = exponent_of(jnp.maximum(bound[...], largest))


def half_pieces(ao_ints, vir_coef, core, sizes):
    naos, aux = ao_ints.shape
    virtuals = vir_coef.shape[1]
    panel = aux // 4
    shapes = [pltpu.VMEM((8 * s // TILE + 1, TILE, virtuals), jnp.float32) for s in sizes]
    bound = pltpu.VMEM((8, virtuals), jnp.float32)
    in_vmem = pl.BlockSpec(memory_space=pltpu.VMEM)
    cost = pl.CostEstimate(flops=naos * aux * virtuals, bytes_accessed=naos * aux + 2 * aux * virtuals, transcendentals=0)
    limit = pltpu.CompilerParams(vmem_limit_bytes=5 * 2**20)
    source = pltpu.with_memory_space_constraint(ao_ints, pltpu.HBM)
    away = pl.pallas_call(
        functools.partial(half_first_kernel, sizes),
        grid_spec=pltpu.PrefetchScalarGridSpec(
            num_scalar_prefetch=1,
            grid=(2,),
            in_specs=[
                pl.BlockSpec((naos, virtuals), lambda i, b: (0, 0)),
                pl.BlockSpec((naos, panel), lambda i, b: (0, 2 * i + b[0])),
            ],
            out_specs=[in_vmem] * len(shapes),
            scratch_shapes=[bound],
        ),
        out_shape=shapes,
        compiler_params=limit,
        cost_estimate=cost,
    )((1 - core).reshape(1).astype(jnp.int32), pltpu.with_memory_space_constraint(vir_coef, pltpu.HBM), source)
    def rest():
        return pl.pallas_call(
            functools.partial(half_rest_kernel, sizes),
            grid_spec=pltpu.PrefetchScalarGridSpec(
                num_scalar_prefetch=1,
                grid=(2,),
                in_specs=[
                    pl.BlockSpec((naos, virtuals), lambda i, b: (0, 0)),
                    pl.BlockSpec((naos, panel), lambda i, b: (0, 2 * i + b[0])),
                ],
                out_specs=[in_vmem] * (len(shapes) + 1),
            ),
            out_shape=shapes + [bound],
            compiler_params=limit,
            cost_estimate=cost,
        )(core.reshape(1).astype(jnp.int32), pltpu.with_memory_space_constraint(vir_coef, pltpu.HBM), source)

    return away, rest


def exponent_of(bound):
    return jnp.ceil(jnp.log2(jnp.maximum(bound, 1e-30))) + 1.0


def packed(value, exponent):
    head = lax.broadcasted_iota(jnp.int32, value.shape, 0) == value.shape[0] - 1
    return jnp.where(head, exponent, value * jnp.exp2(14.0 - exponent)).astype(jnp.float16)


def exponent_in(message):
    return message[-1, :1].astype(jnp.float32)


def risen(level, messages):
    for message in messages:
        level = jnp.maximum(level, exponent_in(message))
    return level + 1.0


def joined(kept, message, start, tiles):
    mine = lax.dynamic_slice_in_dim(kept, start, tiles + 1, 0)
    theirs = lax.dynamic_slice_in_dim(message, start, tiles + 1, 0).astype(jnp.float32)
    return mine + theirs * jnp.exp2(exponent_in(message) - 14.0)


def row_start(place, rows, piece, sizes):
    half = 2 * sum(sizes)
    return pl.multiple_of(place // 2 * half + 2 * sum(sizes[:piece]) + place % 2 * rows, TILE)


def blocks_of(sizes, places, array, first, count):
    blocks, at = [], 0
    for n in range(count):
        for piece, rows in enumerate(sizes):
            blocks.append((array, at, rows, row_start(places[first + n], rows, piece, sizes)))
            at += rows
    return blocks


def steps_of(sizes):
    cuts = []
    for rows in sizes:
        count = max(1, round(3 * rows / sum(sizes)))
        edges = [rows * n // count // TILE * TILE for n in range(count)] + [rows]
        cuts.append(tuple(zip(edges[:-1], edges[1:])))
    return cuts


def step_rows(sizes):
    return max(b - a for cuts in steps_of(sizes) for a, b in cuts)


def gram_steps(sizes, scale, blocks, cols, out, buffers, sems, beside=()):
    copies = []
    cuts = steps_of(sizes)
    for ref, at, height, start in blocks:
        for a, b in cuts[sizes.index(height)]:
            n = len(copies)
            if n >= SLOTS:
                copies[n - SLOTS].wait()
            slot = n % SLOTS
            buffers[slot, : b - a] = contract_second(ref[at + a : at + b], cols[...]) * scale
            where = pl.ds(pl.multiple_of(start + a, TILE), b - a)
            copies.append(pltpu.make_async_copy(buffers.at[slot, pl.ds(0, b - a)], out.at[where, :], sems.at[slot]))
            copies[n].start()
            if n < len(beside):
                beside[n]()
    for copy in copies[-SLOTS:]:
        copy.wait()


def gram_first_kernel(sizes, scale, places, pair, near, cols, naf, out, partial, ahead, buffers, rows_in, sems, naf_sems):
    blocks = blocks_of(sizes, (places[0], places[2]), pair, 0, 2)
    terms, loads, at = [], [], 0
    for ref, first, height, row in blocks + blocks_of(sizes, places, near, 1, 1):
        here = rows_in.at[pl.ds(at, height), :]
        loads.append(pltpu.make_async_copy(naf.at[pl.ds(row, height), :], here, naf_sems.at[len(loads)]))
        terms.append((ref, first, at, height))
        at += height
    for _, first, height, row in blocks_of(sizes, places, ahead, 3, 1):
        here = ahead.at[pl.ds(first, height), :]
        loads.append(pltpu.make_async_copy(naf.at[pl.ds(row, height), :], here, naf_sems.at[len(loads)]))
    for load in loads:
        load.start()

    def add(n):
        ref, first, at, height = terms[n]
        loads[n].wait()
        term = contract_first(ref[first : first + height], rows_in[at : at + height])
        partial[...] = term if n == 0 else partial[...] + term

    beside = [functools.partial(add, n) for n in range(len(terms))]
    gram_steps(sizes, scale, blocks, cols, out, buffers, sems, beside)
    for load in loads[len(terms) :]:
        load.wait()


def gram_rest_kernel(sizes, scale, places, near, far, cols, begun, out, buffers, sems):
    blocks = blocks_of(sizes, places, near, 1, 1) + blocks_of(sizes, places, far, 3, 1)
    gram_steps(sizes, scale, blocks, cols, out, buffers, sems)


def gram_first(sizes, places, pair, near, cols, naf_vectors):
    in_vmem = pl.BlockSpec(memory_space=pltpu.VMEM)
    in_hbm = pl.BlockSpec(memory_space=pl.ANY)
    block, virtuals = near.shape
    nnaf = naf_vectors.shape[1]
    return pl.pallas_call(
        functools.partial(gram_first_kernel, sizes, 1.0 / virtuals),
        grid_spec=pltpu.PrefetchScalarGridSpec(
            num_scalar_prefetch=1,
            grid=(),
            in_specs=[in_vmem] * 3 + [in_hbm],
            out_specs=[in_hbm, in_vmem, in_vmem],
            scratch_shapes=[
                pltpu.VMEM((SLOTS, step_rows(sizes), 2 * block), jnp.float32),
                pltpu.VMEM((3 * block, nnaf), jnp.bfloat16),
                pltpu.SemaphoreType.DMA((SLOTS,)),
                pltpu.SemaphoreType.DMA((8,)),
            ],
        ),
        out_shape=[
            jax.ShapeDtypeStruct((4 * block, 2 * block), jnp.float32),
            pltpu.VMEM((virtuals, nnaf), jnp.float32),
            pltpu.VMEM((block, nnaf), jnp.bfloat16),
        ],
        compiler_params=pltpu.CompilerParams(vmem_limit_bytes=18 * 2**20),
        cost_estimate=pl.CostEstimate(flops=8 * block * block * virtuals, bytes_accessed=16 * block * block, transcendentals=0),
    )(places, pair, near, cols, pltpu.with_memory_space_constraint(naf_vectors, pltpu.HBM))


def gram_rest(sizes, places, near, far, cols, begun):
    in_vmem = pl.BlockSpec(memory_space=pltpu.VMEM)
    in_hbm = pl.BlockSpec(memory_space=pl.ANY)
    block, virtuals = far.shape
    return pl.pallas_call(
        functools.partial(gram_rest_kernel, sizes, 1.0 / virtuals),
        grid_spec=pltpu.PrefetchScalarGridSpec(
            num_scalar_prefetch=1,
            grid=(),
            in_specs=[in_vmem, in_vmem, in_vmem, in_hbm],
            out_specs=in_hbm,
            scratch_shapes=[pltpu.VMEM((SLOTS, step_rows(sizes), 2 * block), jnp.float32), pltpu.SemaphoreType.DMA((SLOTS,))],
        ),
        out_shape=jax.ShapeDtypeStruct((4 * block, 2 * block), jnp.float32),
        input_output_aliases={4: 0},
        compiler_params=pltpu.CompilerParams(vmem_limit_bytes=VMEM_LIMIT),
        cost_estimate=pl.CostEstimate(flops=8 * block * block * virtuals, bytes_accessed=16 * block * block, transcendentals=0),
    )(places, near, far, cols, begun)


def naf_kernel(far, ahead, before, out):
    out[...] = before[...] + contract_first(far[...], ahead[...])


def project(far, ahead, before):
    in_vmem = pl.BlockSpec(memory_space=pltpu.VMEM)
    return pl.pallas_call(
        naf_kernel,
        in_specs=[in_vmem] * 3,
        out_specs=in_vmem,
        out_shape=pltpu.VMEM(before.shape, jnp.float32),
        compiler_params=pltpu.CompilerParams(vmem_limit_bytes=5 * 2**20),
        cost_estimate=pl.CostEstimate(flops=2 * far.shape[0] * before.size, bytes_accessed=0, transcendentals=0),
    )(far, ahead, before)


def shards_4x8(ao_ints, vir_coef, naf_vectors):
    virtuals = vir_coef.shape[1]
    row_index = lax.axis_index("row")
    col_index = lax.axis_index("col")
    core, x = row_index % 2, row_index // 2
    y, z0, z1 = col_index % 2, col_index // 2 % 2, col_index // 4
    place = {X: x, Y: y, Z0: z0}
    half = ao_ints.shape[1] // 16
    sizes = (592 * half // 960 // TILE * TILE,)
    sizes += (half - sizes[0],)

    away, kept_pieces = half_pieces(ao_ints, vir_coef, core, sizes)
    arrived = [flipped(p.astype(jnp.float16), (1, 0), (1, 0)) for p in away[::-1]][::-1]
    *kept, exponent = kept_pieces()
    exponent = exponent[:1]

    level = risen(exponent, arrived)
    tiles = [8 * s // TILE for s in sizes]
    for step in range(3):
        sent, left = [], []
        for piece, orders in enumerate(ORDERS):
            tiles[piece] //= 2
            own = jnp.where(core == 0, place[orders[0][step]], place[orders[1][step]])
            other = joined(kept[piece], arrived[piece], (1 - own) * tiles[piece], tiles[piece])
            out = packed(other, level)
            if piece == 0:
                kept[1], arrived[1], out = lax.optimization_barrier((kept[1], arrived[1], out))
            sent.append(flipped(out, orders[0][step], orders[1][step]))
            k, m, _ = lax.optimization_barrier((kept[piece], arrived[piece], out))
            left.append(joined(k, m, own * tiles[piece], tiles[piece]))
        kept, arrived = left, sent
        level = risen(level, arrived)

    last = [packed(joined(k, m, 0, n), level) for k, m, n in zip(kept, arrived, tiles)]
    mine = jnp.concatenate([last[0][:-1], last[1]], axis=0)
    theirs = flipped(mine, Z1, Z1)
    places = jnp.stack([2 * (i ^ y) + (j ^ z0) for i in range(2) for j in range(2)]).astype(jnp.int32)
    terms = [m[:-1].astype(jnp.float32) * jnp.exp2(exponent_in(m) - 14.0) for m in (mine, theirs)]
    own = (terms[0] + terms[1]).astype(jnp.bfloat16).reshape(-1, virtuals)
    block = sum(sizes)

    def place_of(x, core, z1, z0, y):
        return (x * 2 + core) * 8 + z1 * 4 + z0 * 2 + y

    corners = [(a, b, c) for a in range(2) for b in range(2) for c in range(2)]
    over_x = [(place_of(a, b, a, b, c), place_of(1 - a, b, a, b, c)) for a, b, c in corners]
    over_x += [(place_of(a, b, a, 1 - b, c), place_of(1 - a, 1 - b, a, b, c)) for a, b, c in corners]
    near = flipped(own, Z0, Z0)
    from_x = lax.ppermute(own, AXES, over_x)
    side = flipped(own, Y, Y)
    pair = jnp.concatenate([own, side], axis=0)
    from_x, near, pair = lax.optimization_barrier((from_x, near, pair))
    here = jnp.where(x == z1, own, from_x)
    there = jnp.where(x == z1, near, from_x)
    mine = jnp.where(z0 == 0, jnp.concatenate([here, there], axis=0), jnp.concatenate([there, here], axis=0))
    theirs = flipped(mine, (1, 0), (1, 0))
    far = flipped(near, Y, Y)
    first_mine = (core == z0) == ((z0 == 0) | (x == z1))
    second_mine = (core == z0) == ((z0 == 1) | (x == z1))
    halves = jnp.where(first_mine, mine[:block], theirs[:block]), jnp.where(second_mine, mine[block:], theirs[block:])
    cuts = (0, sizes[0]), (sizes[0], block)
    columns = jnp.concatenate([half[a:b] for a, b in cuts for half in halves], axis=0)

    gram, partial, ahead = gram_first(sizes, places, pair, near, columns, naf_vectors)
    far, gram = lax.optimization_barrier((far, gram))
    partial = project(far, ahead, partial)
    partial = partial.reshape(4, virtuals // 4, -1)
    share = lambda flip: lax.dynamic_index_in_dim(partial, row_index ^ flip, 0, keepdims=False)
    parts = [flipped(share(flip), (flip, 0), (flip, 0)) for flip in (2, 1, 3)]
    gram = gram_rest(sizes, places, near, far, columns, gram)
    parts, gram = lax.optimization_barrier((parts, gram))
    naf_ints = share(0) + parts[0] + parts[1] + parts[2]
    return gram, naf_ints


def solution(mesh):
    in_specs = (P(("row", "col"), None), P(("row", "col"), None), P("row", "col"))
    out_specs = (P("row", "col"), P("row", "col"))
    plan = shards_4x8 if (mesh.shape["row"], mesh.shape["col"]) == (4, 8) else shards
    return jax.shard_map(plan, mesh=mesh, in_specs=in_specs, out_specs=out_specs, check_vma=False)
```
